32 devices in a mesh: front: 4 (over y, core), panel: 8 (over z, x).
Axes of the slice: x: 2, y: 2, z: 4, core: 2. Of those that a mesh axis runs over, the one named last changes fastest.
Arguments:
- lower_panel: bfloat16 [4, 2, 4096, 4096], P('front', None, 'panel'), may hold values from -0.046875 to 0.046875
- inverse_cols: bfloat16 [4, 2, 4096, 512], P('front', None, 'panel'), may hold values from -0.1875 to 0.1875
- update_panel: bfloat16 [4, 2, 4096, 4096], P('front', None, 'panel'), may hold values from -0.046875 to 0.046875
- pivot_rhs: bfloat16 [4, 2, 128, 4096], P('front', None, None, 'panel'), may hold values from -6 to 6
- update_rhs: bfloat16 [4, 2, 128, 4096], P('front', None, None, 'panel'), may hold values from -6 to 6
- row_maps: int32 [4, 4096], replicated, may hold values from 0 to 8191, as said below
- parent_rhs: float32 [4, 2, 128, 4096], P('front', None, None, 'panel'), may hold values from -6 to 6
Outputs:
- solved: bfloat16 [4, 2, 128, 4096], P('front', None, None, 'panel')
- parent_out: float32 [4, 2, 128, 4096], P('front', None, None, 'panel')
The draws below stay inside these ranges and needn't reach their ends.
Inputs may be any that keep to these rules, and one draw needn't show every extreme that they name: `row_maps`: each row lists 4096 distinct parent rows in increasing order; it always contains 0 and 8191.
All inputs are finite; a program needn't handle non-finite values.
Results may differ from the reference program's by a relative error of at most 0.019.
Values may be sent and summed in bfloat16 or wider, within the bound.
No kernel may reach another device: no remote copies, remote signals or barrier semaphores. Data moves between devices by JAX's collectives and lax.ppermute only.
A program may use at most 64 MiB of HBM per device.

```python
import jax
import jax.numpy as jnp
from jax import lax

P_SIZE = 4096
U = 4096
CB = 512
S = 128
FRONTS = 4
PARENTS = 2
N_PANEL = 8


def draw_row_maps(key, part):
    key = jax.random.fold_in(key, 7)

    def one_front(front_number):
        front_key = jax.random.fold_in(key, front_number)
        chosen = jax.random.permutation(front_key, 2 * U - 2)[:U - 2] + 1
        listed = jnp.concatenate([jnp.zeros((1,), jnp.int32), chosen.astype(jnp.int32), jnp.full((1,), 2 * U - 1, jnp.int32)])
        return jnp.sort(listed).astype(jnp.int32)
    return jax.vmap(one_front)(jnp.arange(FRONTS))


def block_scale(rng, dims, cuts, low, high):
    factor_of = 1.0
    for dim, shards_of in cuts:
        heights = jax.random.uniform(jax.random.fold_in(jax.random.fold_in(rng, 6), dim), (shards_of,), jnp.float32, low / len(cuts), high / len(cuts))
        factor_of = factor_of * jnp.repeat(jnp.exp(heights), dims[dim] // shards_of).reshape((-1,) + (1,) * (len(dims) - 1 - dim))
    return factor_of


def normal_values(key, dims, spread, reach, shards=(), kind=jnp.bfloat16):
    drawn = spread * jax.random.normal(key, dims, jnp.float32)
    if shards:
        drawn = drawn * block_scale(key, dims, shards, -0.22, 0.18)
    return jnp.clip(drawn, -reach, reach).astype(kind)


def setup_inputs(seed: int = 0) -> dict:
    splits = jax.random.split(jax.random.key(seed), 8)
    lower_panel = normal_values(splits[0], (FRONTS, 2, P_SIZE, P_SIZE), (4 * P_SIZE) ** -0.5, 0.046875, ((0, 4), (2, 8)))
    inverse_cols = normal_values(splits[1], (FRONTS, 2, P_SIZE, CB), (2 * CB) ** -0.5, 0.1875, ((0, 4), (2, 8)))
    update_panel = normal_values(splits[2], (FRONTS, 2, U, P_SIZE), (4 * P_SIZE) ** -0.5, 0.046875, ((0, 4), (2, 8)))
    pivot_rhs = normal_values(splits[3], (FRONTS, 2, S, P_SIZE), 1.0, 6.0, ((0, 4), (3, 8)))
    update_rhs = normal_values(splits[4], (FRONTS, 2, S, U), 1.0, 6.0, ((0, 4), (3, 8)))
    row_maps = draw_row_maps(jax.random.fold_in(splits[7], 71), 0)
    parent_rhs = normal_values(splits[6], (FRONTS, 2, S, U), 1.0, 6.0, ((0, 4), (3, 8)), jnp.float32)
    return dict(lower_panel=lower_panel, inverse_cols=inverse_cols, update_panel=update_panel, pivot_rhs=pivot_rhs, update_rhs=update_rhs, row_maps=row_maps, parent_rhs=parent_rhs)


def complex_product(matrix, vector, pattern):
    mat_real = matrix[0].astype(jnp.float32)
    mat_imag = matrix[1].astype(jnp.float32)
    vec_real = vector[0].astype(jnp.float32)
    vec_imag = vector[1].astype(jnp.float32)
    real_part = jnp.einsum(pattern, mat_real, vec_real) - jnp.einsum(pattern, mat_imag, vec_imag)
    imag_part = jnp.einsum(pattern, mat_real, vec_imag) + jnp.einsum(pattern, mat_imag, vec_real)
    return jnp.stack([real_part, imag_part])


def solve_front(operands):
    lower_f, inverse_f, update_f, pivot_f, upd_rhs_f = operands
    group_rows = P_SIZE // N_PANEL
    groups = CB // group_rows
    solution = jnp.zeros((2, S, P_SIZE), jnp.float32)
    for block in range(P_SIZE // CB):
        first = block * CB
        residual = pivot_f[:, :, first:first + CB].astype(jnp.float32)
        if block > 0:
            residual = residual - complex_product(lower_f[:, first:first + CB, :first], solution[:, :, :first], "rc,sc->sr")
        residual_b = residual.astype(jnp.bfloat16)
        inverse_block = inverse_f[:, first:first + CB, :].reshape(2, groups, group_rows, CB)
        residual_groups = residual_b.reshape(2, S, groups, group_rows)
        terms = complex_product(inverse_block, residual_groups, "gri,sgr->gsi")
        terms = terms.astype(jnp.bfloat16).astype(jnp.float32)
        block_value = jnp.sum(terms, axis=1).astype(jnp.bfloat16)
        solution = solution.at[:, :, first:first + CB].set(block_value.astype(jnp.float32))
    child_update = (upd_rhs_f.astype(jnp.float32) - complex_product(update_f, solution, "rc,sc->sr")).astype(jnp.bfloat16)
    return solution.astype(jnp.bfloat16), child_update


def reference(lower_panel, inverse_cols, update_panel, pivot_rhs, update_rhs, row_maps, parent_rhs):
    solved, child_update = lax.map(solve_front, (lower_panel, inverse_cols, update_panel, pivot_rhs, update_rhs))
    parents = parent_rhs.reshape(PARENTS, 2, 2, S, U).transpose(0, 2, 3, 1, 4).reshape(PARENTS, 2, S, 2 * U)
    for front_number in range(FRONTS):
        target = front_number // 2
        merged = parents[target].at[:, :, row_maps[front_number]].add(child_update[front_number].astype(jnp.float32))
        parents = parents.at[target].set(merged)
    parent_out = parents.reshape(PARENTS, 2, S, 2, U).transpose(0, 3, 1, 2, 4).reshape(FRONTS, 2, S, U)
    return solved, parent_out
```

```python
import functools

import jax
import jax.numpy as jnp
import numpy as np
from jax import lax
from jax.experimental import pallas as pl
from jax.experimental.pallas import tpu as pltpu
from jax.sharding import PartitionSpec as P

CB = 512
CHUNKS = 2
F32 = jnp.float32
BF16 = jnp.bfloat16

CHAIN = (
    (1, 0, 3, 2, 5, 4, 7, 6),
    (1, 2, 0, 5, 3, 4, 7, 6),
    (1, 0, 3, 2, 5, 4, 7, 6),
    (1, 0, 3, 4, 5, 2, 7, 6),
    (1, 0, 3, 2, 5, 4, 7, 6),
    (1, 0, 3, 2, 5, 6, 7, 4),
    (1, 0, 3, 2, 5, 4, 7, 6),
)
SPREAD = (
    (2, 0, 3, 1, 5, 4, 7, 6),
    (4, 3, 0, 1, 2, 6, 7, 5),
    (6, 5, 4, 0, 2, 1, 7, 3),
    (1, 7, 6, 5, 0, 2, 4, 3),
    (1, 2, 0, 7, 6, 3, 4, 5),
    (3, 0, 4, 1, 2, 7, 5, 6),
    (1, 2, 6, 7, 0, 3, 4, 5),
    (3, 0, 4, 7, 6, 1, 2, 5),
    (1, 2, 4, 5, 6, 7, 0, 3),
    (2, 0, 3, 5, 6, 4, 7, 1),
)
PAIRS = ((0,), (1, 0), (2, 1, 0), (3, 2, 1), (4, 3, 2), (5, 4, 3), (6, 5, 4), (7, 6, 5), (7, 6), (7,))
SWAP = (1, 0, 3, 2, 5, 4, 7, 6)


def pairs_of(dests):
    return [(source, dest) for source, dest in enumerate(dests)]


def spread_plan(count):
    have = [{p, p - 1} for p in range(count)]
    arrivals = []
    for hop, sources in enumerate(PAIRS):
        first = [-1] * count
        second = [-1] * count
        for source in sources:
            dest = SPREAD[hop][source]
            second[dest] = source
            if source != count - 1:
                first[dest] = source - 1
        for p in range(count):
            for block in (first[p], second[p]):
                if block >= 0:
                    assert block not in have[p]
                    have[p].add(block)
        arrivals.append((first, second))
    last = [-1] * count
    for p in range(count):
        block = count - 1 if p % 2 == 0 else count - 2
        if block not in have[p]:
            last[p] = block
            have[p].add(block)
    assert all(held >= set(range(count)) for held in have)
    return arrivals, last


def stacked(value):
    return jnp.concatenate([value[0], value[1]], axis=0)


def turned_of(value):
    half = value.shape[0] // 2
    return jnp.concatenate([-value[half:], value[:half]], axis=0)


def apply_rows(value, matrix_real, matrix_imag):
    dims = (((1,), (1,)), ((), ()))
    return lax.dot_general(value, matrix_real, dims, preferred_element_type=F32) + lax.dot_general(
        turned_of(value), matrix_imag, dims, preferred_element_type=F32
    )


def apply_columns(value, matrix_real, matrix_imag):
    return jnp.dot(value, matrix_real, preferred_element_type=F32) + jnp.dot(
        turned_of(value), matrix_imag, preferred_element_type=F32
    )


def weights_kernel(place_ref, lower_ref, inverse_ref, near_ref, inv_ref, sems):
    width = near_ref.shape[-1]
    block = jnp.maximum(place_ref[0] - 1, 0)
    columns = pl.ds(pl.multiple_of(block * width, width), width)
    copies = (
        pltpu.make_async_copy(lower_ref.at[0, :, :, columns], near_ref, sems.at[0]),
        pltpu.make_async_copy(inverse_ref.at[0], inv_ref, sems.at[1]),
    )
    for copy in copies:
        copy.start()
    for copy in copies:
        copy.wait()


def resident_weights(place, lower, inverse):
    rows = lower.shape[2]
    hbm = pl.BlockSpec(memory_space=pl.ANY)
    vmem = pl.BlockSpec(memory_space=pltpu.VMEM)
    return pl.pallas_call(
        weights_kernel,
        out_shape=(pltpu.VMEM((2, rows, CB), BF16), pltpu.VMEM((2, rows, CB), BF16)),
        in_specs=[pl.BlockSpec(memory_space=pltpu.SMEM), hbm, hbm],
        out_specs=(vmem, vmem),
        scratch_shapes=[pltpu.SemaphoreType.DMA((2,))],
        name="weights",
    )(place, lower, inverse)


def solve_kernel(hop, chunk, place_ref, rhs_ref, acc_ref, urgent_ref, near_ref, inv_ref, out_ref):
    shots = out_ref.shape[1]
    piece = slice(chunk * shots, (chunk + 1) * shots)

    @pl.when(place_ref[0] != hop)
    def _():
        out_ref[...] = jnp.zeros_like(out_ref)

    @pl.when(place_ref[0] == hop)
    def _():
        residual = stacked(rhs_ref[:, piece]).astype(F32)
        if hop > 0:
            residual = residual - stacked(acc_ref[:, piece])
            residual = residual - apply_rows(stacked(urgent_ref[...]), near_ref[0], near_ref[1])
        term = apply_columns(residual.astype(BF16), inv_ref[0], inv_ref[1]).astype(BF16)
        out_ref[0] = term[:shots]
        out_ref[1] = term[shots:]


def solve(hop, chunk, place, rhs, acc, urgent, near, inv):
    vmem = pl.BlockSpec(memory_space=pltpu.VMEM)
    return pl.pallas_call(
        functools.partial(solve_kernel, hop, chunk),
        out_shape=jax.ShapeDtypeStruct(urgent.shape, BF16),
        in_specs=[pl.BlockSpec(memory_space=pltpu.SMEM)] + [vmem] * 5,
        out_specs=vmem,
        compiler_params=pltpu.CompilerParams(vmem_limit_bytes=16 * 2**20),
        name=f"solve_{hop}_{chunk}",
    )(place, rhs, acc, urgent, near, inv)


def gather_kernel(left, table_ref, *refs):
    count = len(left)
    parts = refs[:count]
    lower_ref, update_ref, acc_l_in, acc_u_in, acc_l_ref, acc_u_ref, buf_l, buf_u, sems = refs[count:]
    width = buf_l.shape[-1]
    shots = acc_l_ref.shape[1]
    place = table_ref[0]

    def copy_of(i, panel_ref, buf, which):
        block = jnp.maximum(table_ref[1 + i], 0)
        columns = pl.ds(pl.multiple_of(block * width, width), width)
        return pltpu.make_async_copy(panel_ref.at[0, :, :, columns], buf.at[i], sems.at[i, which])

    def when_update(i):
        return table_ref[1 + i] >= 0

    def when_lower(i):
        return jnp.logical_and(table_ref[1 + i] >= 0, table_ref[1 + i] < place)

    for i in range(count):
        if left[i]:

            @pl.when(when_lower(i))
            def _(i=i):
                copy_of(i, lower_ref, buf_l, 0).start()

        @pl.when(when_update(i))
        def _(i=i):
            copy_of(i, update_ref, buf_u, 1).start()

    acc_l_ref[...] = acc_l_in[...]
    acc_u_ref[...] = acc_u_in[...]

    def add(i, copy, buf, acc_ref):
        copy.wait()
        product = apply_rows(stacked(parts[i][...]), buf[i, 0], buf[i, 1])
        acc_ref[0] += product[:shots]
        acc_ref[1] += product[shots:]

    for i in range(count):
        if left[i]:

            @pl.when(when_lower(i))
            def _(i=i):
                add(i, copy_of(i, lower_ref, buf_l, 0), buf_l, acc_l_ref)

        @pl.when(when_update(i))
        def _(i=i):
            add(i, copy_of(i, update_ref, buf_u, 1), buf_u, acc_u_ref)


def accumulate(name, table, parts, left, lower, update, acc_l, acc_u):
    count = len(parts)
    vmem = pl.BlockSpec(memory_space=pltpu.VMEM)
    hbm = pl.BlockSpec(memory_space=pl.ANY)
    rows = lower.shape[2]
    shape = jax.ShapeDtypeStruct(acc_l.shape, F32)
    return pl.pallas_call(
        functools.partial(gather_kernel, left),
        out_shape=(shape, shape),
        in_specs=[pl.BlockSpec(memory_space=pltpu.SMEM)] + [vmem] * count + [hbm, hbm, vmem, vmem],
        out_specs=(vmem, vmem),
        scratch_shapes=[
            pltpu.VMEM((count, 2, rows, CB), BF16),
            pltpu.VMEM((count, 2, rows, CB), BF16),
            pltpu.SemaphoreType.DMA((count, 2)),
        ],
        input_output_aliases={count + 3: 0, count + 4: 1},
        compiler_params=pltpu.CompilerParams(vmem_limit_bytes=24 * 2**20),
        name=name,
    )(table, *parts, lower, update, acc_l, acc_u)


def place_kernel(own_ref, other_ref, own_hot_ref, other_hot_ref, *out_refs):
    own = stacked(own_ref[...])
    other = stacked(other_ref[...])
    shots = own_ref.shape[1]
    for i, out_ref in enumerate(out_refs):
        rows = jnp.dot(own, own_hot_ref[i], preferred_element_type=F32) + jnp.dot(
            other, other_hot_ref[i], preferred_element_type=F32
        )
        rows = rows.astype(BF16)
        out_ref[0] = rows[:shots]
        out_ref[1] = rows[shots:]


def place_rows(own, other, own_hot, other_hot):
    vmem = pl.BlockSpec(memory_space=pltpu.VMEM)
    shape = jax.ShapeDtypeStruct(own.shape, BF16)
    count = own_hot.shape[0]
    return pl.pallas_call(
        place_kernel,
        out_shape=(shape,) * count,
        in_specs=[vmem] * 4,
        out_specs=(vmem,) * count,
        compiler_params=pltpu.CompilerParams(vmem_limit_bytes=24 * 2**20),
        name="place_rows",
    )(own, other, own_hot, other_hot)


def placements(row_maps, place, count, rows):
    own_map = lax.dynamic_index_in_dim(row_maps, lax.axis_index("front"), 0, keepdims=False)
    level = place // 2
    firsts = [place * rows, (count + place) * rows]
    for step in range(1, count // 2):
        far = level ^ step
        target = 2 * far + place % 2
        firsts.append(jnp.where(far < level, count + target, target) * rows)
    firsts = jnp.stack(firsts)
    targets = firsts[:, None] + jnp.arange(rows, dtype=jnp.int32)[None, :]

    def hot(device):
        mapped = lax.dynamic_slice_in_dim(own_map, device * rows, rows, 0)
        return (mapped[None, :, None] == targets[:, None, :]).astype(BF16)

    return hot(place), hot(place ^ 1)


def relay_body(lower_panel, inverse_cols, update_panel, pivot_rhs, update_rhs, row_maps, parent_rhs):
    pivot_f = pivot_rhs[0]
    shots, own_rows = pivot_f.shape[1:]
    upd_rows = update_panel.shape[2]
    count = lax.axis_size("panel")
    place = lax.axis_index("panel").astype(jnp.int32)
    level = place // 2
    arrivals, last = spread_plan(count)
    piece = shots // CHUNKS

    def send(value, dests):
        return lax.ppermute(value, "panel", pairs_of(dests))

    def table(*rows):
        columns = np.array([list(range(count)), *rows], np.int32)
        return lax.dynamic_index_in_dim(jnp.asarray(columns), place, 1, keepdims=False)

    def only(hop, block):
        return [block if p == hop else -1 for p in range(count)]

    place_ref = jnp.reshape(place, (1,))
    own_hot, other_hot = placements(row_maps, place, count, upd_rows)
    near, inv = resident_weights(place_ref, lower_panel, inverse_cols)
    acc_l = jnp.zeros((2, shots, own_rows), F32)
    acc_u = jnp.zeros((2, shots, upd_rows), F32)
    mine = jnp.zeros((2, shots, CB), BF16)
    before = mine
    urgent = [jnp.zeros((2, piece, CB), BF16)] * CHUNKS
    got = None
    for hop in range(count):
        fresh = [solve(hop, i, place_ref, pivot_f, acc_l, urgent[i], near, inv) for i in range(CHUNKS)]
        arrived = urgent
        if hop + 1 < count:
            urgent = [send(value, CHAIN[hop]) for value in fresh]
        here = place == hop
        before = jnp.where(here, jnp.concatenate(arrived, axis=1), before)
        mine = jnp.where(here, jnp.concatenate(fresh, axis=1), mine)
        if got is None:
            parts = [mine]
            blocks = [only(hop, hop)]
            left = (False,)
        else:
            parts = [before, mine, *got]
            blocks = [only(hop, hop - 1), only(hop, hop), *arrivals[hop - 1]]
            left = (False, False, True, True)
        spread = [send(before, SPREAD[hop]), send(mine, SPREAD[hop])]
        acc_l, acc_u = accumulate(
            f"accumulate_{hop}", table(*blocks), parts, left, lower_panel, update_panel, acc_l, acc_u
        )
        previous, got = got, spread
    late = [send(before, SPREAD[count]), send(mine, SPREAD[count])]
    latest = send(mine, SPREAD[count + 1])
    crossing = mine
    for p, value in ((0, late[1]), (1, latest), (2, got[1]), (3, late[1]), (4, previous[1]), (5, got[1])):
        crossing = jnp.where(place == p, value, crossing)
    crossed = send(crossing, SWAP)
    blocks = [*arrivals[count - 1], *arrivals[count], arrivals[count + 1][1]]
    acc_l, acc_u = accumulate(
        "accumulate_late", table(*blocks), [*got, *late, latest], (False,) * 5, lower_panel, update_panel, acc_l, acc_u
    )
    acc_l, acc_u = accumulate(
        "accumulate_last", table(last), [crossed], (False,), lower_panel, update_panel, acc_l, acc_u
    )
    child = (update_rhs[0].astype(F32) - acc_u).astype(BF16)
    other = send(child, SWAP)
    placed = place_rows(child, other, own_hot, other_hot)
    sums = [placed[0].astype(F32), placed[1].astype(F32)]
    for step in range(1, count // 2):
        came = send(placed[1 + step], [p ^ (2 * step) for p in range(count)]).astype(F32)
        below = (level ^ step) < level
        sums[0] = sums[0] + jnp.where(below, came, 0.0)
        sums[1] = sums[1] + jnp.where(below, 0.0, came)
    second = lax.axis_index("front") % 2 == 1
    kept = jnp.where(second, sums[1], sums[0])
    given = jnp.where(second, sums[0], sums[1]).astype(BF16)
    sibling = lax.ppermute(given, "front", [(f, f ^ 1) for f in range(lax.axis_size("front"))])
    parent_out = parent_rhs[0] + kept + sibling.astype(F32)
    return (mine[None], parent_out[None])


def select_rows(block_rows, index_map, base, owned):
    targets = base + jnp.arange(owned, dtype=jnp.int32)
    placement = (index_map[:, None] == targets[None, :]).astype(BF16)
    return jnp.einsum("csu,ur->csr", block_rows, placement, preferred_element_type=F32)


def extend_add(child_update, row_maps, parent_f):
    upd_rows = child_update.shape[2]
    panel_count = lax.axis_size("panel")
    panel_number = lax.axis_index("panel")
    front_number = lax.axis_index("front")
    parity = front_number % 2
    sibling_front = front_number + 1 - 2 * parity
    my_base = (parity * panel_count + panel_number) * upd_rows
    own_map = lax.dynamic_index_in_dim(row_maps, front_number, 0, keepdims=False)
    sibling_map = lax.dynamic_index_in_dim(row_maps, sibling_front, 0, keepdims=False)
    gathered = lax.all_gather(child_update, "panel", axis=2, tiled=True)
    pairs = [(source, source ^ 1) for source in range(lax.axis_size("front"))]
    sibling = lax.ppermute(gathered, "front", pairs)
    assembled = select_rows(gathered, own_map, my_base, upd_rows) + select_rows(
        sibling, sibling_map, my_base, upd_rows
    )
    return parent_f + assembled


def complex_product(matrix, vector, pattern):
    real_part = jnp.einsum(pattern, matrix[0], vector[0], preferred_element_type=F32) - jnp.einsum(
        pattern, matrix[1], vector[1], preferred_element_type=F32
    )
    imag_part = jnp.einsum(pattern, matrix[0], vector[1], preferred_element_type=F32) + jnp.einsum(
        pattern, matrix[1], vector[0], preferred_element_type=F32
    )
    return jnp.stack([real_part, imag_part])


def summed_body(lower_panel, inverse_cols, update_panel, pivot_rhs, update_rhs, row_maps, parent_rhs):
    lower_f = lower_panel[0]
    pivot_f = pivot_rhs[0]
    own_rows = lower_f.shape[1]
    block_count = lower_f.shape[2] // CB
    panel_number = lax.axis_index("panel")
    owner_block = panel_number * own_rows // CB
    partial_sum = jnp.zeros((2, pivot_f.shape[1], own_rows), F32)
    blocks = []
    for block in range(block_count):
        first = block * CB
        residual = (pivot_f.astype(F32) - partial_sum).astype(BF16)
        block_term = complex_product(inverse_cols[0], residual, "ri,sr->si")
        block_term = jnp.where(owner_block == block, block_term, 0.0)
        block_value = lax.psum(block_term.astype(BF16), "panel")
        blocks.append(block_value)
        partial_sum = partial_sum + complex_product(lower_f[:, :, first : first + CB], block_value, "rc,sc->sr")
    solution_f = jnp.concatenate(blocks, axis=2)
    own_solution = lax.dynamic_slice_in_dim(solution_f, panel_number * own_rows, own_rows, 2)
    applied = complex_product(update_panel[0], solution_f, "rc,sc->sr")
    child_update = (update_rhs[0].astype(F32) - applied).astype(BF16)
    parent_out = extend_add(child_update, row_maps, parent_rhs[0])
    return (own_solution[None], parent_out[None])


def solution(mesh):
    in_specs = (
        P("front", None, "panel", None),
        P("front", None, "panel", None),
        P("front", None, "panel", None),
        P("front", None, None, "panel"),
        P("front", None, None, "panel"),
        P(),
        P("front", None, None, "panel"),
    )
    out_specs = (P("front", None, None, "panel"), P("front", None, None, "panel"))

    def run(lower_panel, *others):
        blocks = lower_panel.shape[3] // CB
        one_block = mesh.shape["panel"] == blocks == len(SWAP)
        body = relay_body if one_block else summed_body
        call = jax.shard_map(body, mesh=mesh, in_specs=in_specs, out_specs=out_specs, check_vma=False)
        return call(lower_panel, *others)

    return run
```

```python
import functools

import jax
import jax.numpy as jnp
import numpy as np
from jax import lax
from jax.experimental import pallas as pl
from jax.experimental.pallas import tpu as pltpu
from jax.sharding import PartitionSpec as P

CB = 512
F32 = jnp.float32
BF16 = jnp.bfloat16

SWAP = ((0, 1), (1, 0), (2, 3), (3, 2), (4, 5), (5, 4), (6, 7), (7, 6))
CHAIN = (SWAP, ((1, 2),), SWAP, ((3, 4),), SWAP, ((5, 6),), SWAP)
RELAY = {2: {4: (0, 1), 6: (0, 2)}, 4: {6: (2, 2), 7: (2, 3)}, 6: {0: (4, 3), 1: (4, 2)}}
SPREAD = (
    ((True, ((0, 2),), 1), (True, ((0, 4),), 3), (True, ((0, 6),), 5)),
    ((False, ((1, 3),), 2), (True, ((1, 3),), 2), (True, ((1, 5),), 4)),
    ((False, ((2, 4),), 3), (True, ((2, 4),), 3), (True, ((2, 6),), 5), (True, ((1, 7),), 6)),
    ((False, ((3, 5),), 4), (True, ((3, 5),), 4)),
    ((False, ((4, 6),), 5), (True, ((4, 6), (3, 7)), 5), (True, ((3, 1),), 7), (True, ((2, 0),), 7)),
    ((False, ((5, 7),), 6), (True, ((5, 7), (4, 2)), 6)),
    (
        (True, ((6, 4), (5, 3), (4, 0)), 7),
        (True, ((6, 2), (5, 1)), 7),
        (True, ((6, 0),), 7),
        (False, ((5, 3),), 7),
        (False, ((5, 1),), 7),
    ),
    ((True, ((7, 5),), 8), (True, ((7, 3),), 8), (True, ((7, 1),), 8)),
)


def spread_plan(count):
    have = [{p} for p in range(count)]

    def taken(edges, block_of):
        row = [-1] * count
        for source, dest in edges:
            block = block_of(source)
            if block is not None and block not in have[dest]:
                row[dest] = block
        return row

    def keep(row):
        for p, block in enumerate(row):
            if block >= 0:
                assert block not in have[p]
                have[p].add(block)

    chain = []
    spread = []
    for hop in range(count):
        if hop < len(CHAIN):

            def passed(p, hop=hop):
                if p in RELAY.get(hop, {}):
                    earlier, i = RELAY[hop][p]
                    return spread[earlier][i][p]
                return p if p <= hop else None

            row = taken(CHAIN[hop], passed)
            assert row[hop + 1] == hop
            keep(row)
            chain.append(row)
        rows = []
        for own, edges, _ in SPREAD[hop]:
            row = taken(edges, lambda source, own=own: source if own else source - 1)
            assert sum(block >= 0 for block in row) == len(edges)
            keep(row)
            rows.append(row)
        spread.append(rows)
    swaps = []
    for even, odd in ((count - 3, count - 2), (count - 1, None)):
        row = taken(SWAP, lambda source, even=even, odd=odd: even if source % 2 else odd)
        keep(row)
        swaps.append(row)
    assert all(held == set(range(count)) for held in have)
    for p in range(count):
        for hop, rows in enumerate(spread):
            for (_, _, use), row in zip(SPREAD[hop], rows):
                assert use > hop and (row[p] < 0 or row[p] > p or use < p)
        for hop, row in enumerate(chain):
            assert row[p] < 0 or row[p] > p or hop + 1 < p or (hop + 1 == p and row[p] == hop)
    return spread, chain, swaps


def stacked(value):
    return jnp.concatenate([value[0], value[1]], axis=0)


def turned_of(value):
    half = value.shape[0] // 2
    return jnp.concatenate([-value[half:], value[:half]], axis=0)


def apply_rows(value, matrix_real, matrix_imag):
    dims = (((1,), (1,)), ((), ()))
    return lax.dot_general(value, matrix_real, dims, preferred_element_type=F32) + lax.dot_general(
        turned_of(value), matrix_imag, dims, preferred_element_type=F32
    )


def apply_columns(value, matrix_real, matrix_imag):
    return jnp.dot(value, matrix_real, preferred_element_type=F32) + jnp.dot(
        turned_of(value), matrix_imag, preferred_element_type=F32
    )


def setup_kernel(place_ref, lower_ref, inverse_ref, pivot_ref, near_ref, inv_ref, rhs_ref, acc_l_ref, acc_u_ref, mine_ref, before_ref, sems):
    width = near_ref.shape[-1]
    block = jnp.maximum(place_ref[0] - 1, 0)
    columns = pl.ds(pl.multiple_of(block * width, width), width)
    copies = (
        pltpu.make_async_copy(pivot_ref.at[0], rhs_ref, sems.at[0]),
        pltpu.make_async_copy(inverse_ref.at[0], inv_ref, sems.at[1]),
        pltpu.make_async_copy(lower_ref.at[0, :, :, columns], near_ref, sems.at[2]),
    )
    for copy in copies:
        copy.start()
    for ref in (acc_l_ref, acc_u_ref, mine_ref, before_ref):
        ref[...] = jnp.zeros_like(ref)
    for copy in copies:
        copy.wait()


def setup(place, lower, inverse, pivot):
    rows = lower.shape[2]
    shots = pivot.shape[2]
    hbm = pl.BlockSpec(memory_space=pltpu.HBM)
    vmem = pl.BlockSpec(memory_space=pltpu.VMEM)
    weight = pltpu.VMEM((2, rows, CB), BF16)
    block = pltpu.VMEM((2, shots, CB), BF16)
    acc = pltpu.VMEM((2, shots, rows), F32)
    return pl.pallas_call(
        setup_kernel,
        out_shape=(weight, weight, block, acc, acc, block, block),
        in_specs=[pl.BlockSpec(memory_space=pltpu.SMEM), hbm, hbm, hbm],
        out_specs=(vmem,) * 7,
        scratch_shapes=[pltpu.SemaphoreType.DMA((3,))],
        compiler_params=pltpu.CompilerParams(vmem_limit_bytes=46 * 2**20),
        name="setup",
    )(place, lower, inverse, pivot)


def solve_kernel(hop, relays, place_ref, rhs_ref, acc_ref, near_ref, inv_ref, urgent_ref, mine_in, before_in, *refs):
    relay_refs, (out_ref, mine_ref, before_ref) = refs[: len(relays)], refs[len(relays) :]
    place = place_ref[0]
    shots = out_ref.shape[1]

    @pl.when(place != hop)
    def _():
        out_ref[...] = mine_in[...]
        mine_ref[...] = mine_in[...]
        before_ref[...] = before_in[...]

    for p, relay_ref in zip(relays, relay_refs):

        @pl.when(place == p)
        def _(relay_ref=relay_ref):
            out_ref[...] = relay_ref[...]

    @pl.when(place == hop)
    def _():
        residual = stacked(rhs_ref[...]).astype(F32)
        if hop > 0:
            residual = residual - stacked(acc_ref[...])
            residual = residual - apply_rows(stacked(urgent_ref[...]), near_ref[0], near_ref[1])
        term = apply_columns(residual.astype(BF16), inv_ref[0], inv_ref[1]).astype(BF16)
        for ref in (out_ref, mine_ref):
            ref[0] = term[:shots]
            ref[1] = term[shots:]
        before_ref[...] = urgent_ref[...]


def solve(hop, place, rhs, acc, near, inv, urgent, mine, before, relays):
    vmem = pl.BlockSpec(memory_space=pltpu.VMEM)
    smem = pl.BlockSpec(memory_space=pltpu.SMEM)
    block = pltpu.VMEM(mine.shape, BF16)
    args = [rhs, acc, near, inv, urgent, mine, before, *relays.values()]
    return pl.pallas_call(
        functools.partial(solve_kernel, hop, tuple(relays)),
        out_shape=(block,) * 3,
        in_specs=[smem] + [vmem] * len(args),
        out_specs=(vmem,) * 3,
        compiler_params=pltpu.CompilerParams(vmem_limit_bytes=16 * 2**20),
        name=f"solve_{hop}",
    )(place, *args)


def gather_kernel(arrivals, left, place_ref, *refs):
    count = len(left)
    parts = refs[:count]
    lower_ref, update_ref, acc_l_in, acc_u_in, acc_l_ref, acc_u_ref, buf_l, buf_u, sems = refs[count:]
    width = buf_l.shape[-1]
    shots = acc_l_ref.shape[1]
    place = place_ref[0]
    blocks = []
    for row in arrivals:
        block = jnp.int32(-1)
        for p, value in enumerate(row):
            if value >= 0:
                block = jnp.where(place == p, value, block)
        blocks.append(block)

    def copy_of(i, panel_ref, buf, which):
        block = jnp.maximum(blocks[i], 0)
        columns = pl.ds(pl.multiple_of(block * width, width), width)
        return pltpu.make_async_copy(panel_ref.at[0, :, :, columns], buf.at[i], sems.at[i, which])

    def when_update(i):
        return blocks[i] >= 0

    def when_lower(i):
        return jnp.logical_and(blocks[i] >= 0, blocks[i] < place)

    for i in range(count):
        if left[i]:

            @pl.when(when_lower(i))
            def _(i=i):
                copy_of(i, lower_ref, buf_l, 0).start()

        @pl.when(when_update(i))
        def _(i=i):
            copy_of(i, update_ref, buf_u, 1).start()

    acc_l_ref[...] = acc_l_in[...]
    acc_u_ref[...] = acc_u_in[...]

    def add(i, copy, buf, acc_ref):
        copy.wait()
        product = apply_rows(stacked(parts[i][...]), buf[i, 0], buf[i, 1])
        acc_ref[0] += product[:shots]
        acc_ref[1] += product[shots:]

    for i in range(count):
        if left[i]:

            @pl.when(when_lower(i))
            def _(i=i):
                add(i, copy_of(i, lower_ref, buf_l, 0), buf_l, acc_l_ref)

        @pl.when(when_update(i))
        def _(i=i):
            add(i, copy_of(i, update_ref, buf_u, 1), buf_u, acc_u_ref)


def accumulate(name, place, items, lower, update, acc_l, acc_u):
    parts = [item[0] for item in items]
    arrivals = [item[1] for item in items]
    left = [item[2] for item in items]
    count = len(parts)
    vmem = pl.BlockSpec(memory_space=pltpu.VMEM)
    hbm = pl.BlockSpec(memory_space=pltpu.HBM)
    rows = lower.shape[2]
    shape = pltpu.VMEM(acc_l.shape, F32)
    return pl.pallas_call(
        functools.partial(gather_kernel, arrivals, left),
        out_shape=(shape, shape),
        in_specs=[pl.BlockSpec(memory_space=pltpu.SMEM)] + [vmem] * count + [hbm, hbm, vmem, vmem],
        out_specs=(vmem, vmem),
        scratch_shapes=[
            pltpu.VMEM((count, 2, rows, CB), BF16),
            pltpu.VMEM((count, 2, rows, CB), BF16),
            pltpu.SemaphoreType.DMA((count, 2)),
        ],
        input_output_aliases={count + 3: 0, count + 4: 1},
        compiler_params=pltpu.CompilerParams(vmem_limit_bytes=46 * 2**20),
        name=name,
    )(place, *parts, lower, update, acc_l, acc_u)


def place_kernel(own_ref, other_ref, own_hot_ref, other_hot_ref, *out_refs):
    own = stacked(own_ref[...])
    other = stacked(other_ref[...])
    shots = own_ref.shape[1]
    for i, out_ref in enumerate(out_refs):
        rows = jnp.dot(own, own_hot_ref[i], preferred_element_type=F32) + jnp.dot(
            other, other_hot_ref[i], preferred_element_type=F32
        )
        rows = rows.astype(BF16)
        out_ref[0] = rows[:shots]
        out_ref[1] = rows[shots:]


def place_rows(own, other, own_hot, other_hot):
    vmem = pl.BlockSpec(memory_space=pltpu.VMEM)
    shape = jax.ShapeDtypeStruct(own.shape, BF16)
    count = own_hot.shape[0]
    return pl.pallas_call(
        place_kernel,
        out_shape=(shape,) * count,
        in_specs=[vmem] * 4,
        out_specs=(vmem,) * count,
        compiler_params=pltpu.CompilerParams(vmem_limit_bytes=24 * 2**20),
        name="place_rows",
    )(own, other, own_hot, other_hot)


def placements(row_maps, place, count, rows):
    own_map = lax.dynamic_index_in_dim(row_maps, lax.axis_index("front"), 0, keepdims=False)
    level = place // 2
    firsts = [place * rows, (count + place) * rows]
    for step in range(1, count // 2):
        far = level ^ step
        target = 2 * far + place % 2
        firsts.append(jnp.where(far < level, count + target, target) * rows)
    firsts = jnp.stack(firsts)
    targets = firsts[:, None] + jnp.arange(rows, dtype=jnp.int32)[None, :]

    def hot(device):
        mapped = lax.dynamic_slice_in_dim(own_map, device * rows, rows, 0)
        return (mapped[None, :, None] == targets[:, None, :]).astype(BF16)

    return hot(place), hot(place ^ 1)


def relay_body(lower_panel, inverse_cols, update_panel, pivot_rhs, update_rhs, row_maps, parent_rhs):
    shots = pivot_rhs.shape[2]
    upd_rows = update_panel.shape[2]
    count = lax.axis_size("panel")
    place = lax.axis_index("panel").astype(jnp.int32)
    level = place // 2
    spread_rows, chain_rows, swap_rows = spread_plan(count)

    def send(value, edges):
        return lax.ppermute(value, "panel", edges)

    place_ref = jnp.reshape(place, (1,))
    own_hot, other_hot = placements(row_maps, place, count, upd_rows)
    near, inv, rhs, acc_l, acc_u, mine, before = setup(place_ref, lower_panel, inverse_cols, pivot_rhs)
    urgent = mine
    came = []
    for hop in range(count):
        relays = {p: came[earlier][i] for p, (earlier, i) in RELAY.get(hop, {}).items()}
        passed, mine, before = solve(hop, place_ref, rhs, acc_l, near, inv, urgent, mine, before, relays)
        parts = [(mine, [hop if p == hop else -1 for p in range(count)], False)]
        if hop:
            parts.append((urgent, chain_rows[hop - 1], True))
        if hop < len(CHAIN):
            urgent = send(passed, CHAIN[hop])
        came.append([send(mine if own else before, edges) for own, edges, _ in SPREAD[hop]])
        for earlier in range(hop):
            for i, (_, _, use) in enumerate(SPREAD[earlier]):
                if use == hop:
                    parts.append((came[earlier][i], spread_rows[earlier][i], True))
        acc_l, acc_u = accumulate(f"accumulate_{hop}", place_ref, parts, lower_panel, update_panel, acc_l, acc_u)

    def cross(blocks):
        value = mine
        for earlier, rows in enumerate(spread_rows):
            for i, row in enumerate(rows):
                for p in range(count):
                    if row[p] == blocks[p % 2]:
                        value = jnp.where(place == p, came[earlier][i], value)
        return send(value, SWAP)

    first = cross((count - 2, count - 3))
    second = cross((None, count - 1))
    parts = [(came[-1][i], row, False) for i, row in enumerate(spread_rows[-1])]
    parts.append((first, swap_rows[0], False))
    acc_l, acc_u = accumulate("accumulate_late", place_ref, parts, lower_panel, update_panel, acc_l, acc_u)
    parts = [(second, swap_rows[1], False)]
    acc_l, acc_u = accumulate("accumulate_last", place_ref, parts, lower_panel, update_panel, acc_l, acc_u)
    child = (update_rhs[0].astype(F32) - acc_u).astype(BF16)
    other = send(child, SWAP)
    placed = place_rows(child, other, own_hot, other_hot)
    sums = [placed[0].astype(F32), placed[1].astype(F32)]
    for step in range(1, count // 2):
        moved = send(placed[1 + step], [(p, p ^ (2 * step)) for p in range(count)]).astype(F32)
        below = (level ^ step) < level
        sums[0] = sums[0] + jnp.where(below, moved, 0.0)
        sums[1] = sums[1] + jnp.where(below, 0.0, moved)
    odd_front = lax.axis_index("front") % 2 == 1
    kept = jnp.where(odd_front, sums[1], sums[0])
    given = jnp.where(odd_front, sums[0], sums[1]).astype(BF16)
    sibling = lax.ppermute(given, "front", [(f, f ^ 1) for f in range(lax.axis_size("front"))])
    parent_out = parent_rhs[0] + kept + sibling.astype(F32)
    return (mine[None], parent_out[None])


def select_rows(block_rows, index_map, base, owned):
    targets = base + jnp.arange(owned, dtype=jnp.int32)
    placement = (index_map[:, None] == targets[None, :]).astype(BF16)
    return jnp.einsum("csu,ur->csr", block_rows, placement, preferred_element_type=F32)


def extend_add(child_update, row_maps, parent_f):
    upd_rows = child_update.shape[2]
    panel_count = lax.axis_size("panel")
    panel_number = lax.axis_index("panel")
    front_number = lax.axis_index("front")
    parity = front_number % 2
    sibling_front = front_number + 1 - 2 * parity
    my_base = (parity * panel_count + panel_number) * upd_rows
    own_map = lax.dynamic_index_in_dim(row_maps, front_number, 0, keepdims=False)
    sibling_map = lax.dynamic_index_in_dim(row_maps, sibling_front, 0, keepdims=False)
    gathered = lax.all_gather(child_update, "panel", axis=2, tiled=True)
    pairs = [(source, source ^ 1) for source in range(lax.axis_size("front"))]
    sibling = lax.ppermute(gathered, "front", pairs)
    assembled = select_rows(gathered, own_map, my_base, upd_rows) + select_rows(
        sibling, sibling_map, my_base, upd_rows
    )
    return parent_f + assembled


def complex_product(matrix, vector, pattern):
    real_part = jnp.einsum(pattern, matrix[0], vector[0], preferred_element_type=F32) - jnp.einsum(
        pattern, matrix[1], vector[1], preferred_element_type=F32
    )
    imag_part = jnp.einsum(pattern, matrix[0], vector[1], preferred_element_type=F32) + jnp.einsum(
        pattern, matrix[1], vector[0], preferred_element_type=F32
    )
    return jnp.stack([real_part, imag_part])


def summed_body(lower_panel, inverse_cols, update_panel, pivot_rhs, update_rhs, row_maps, parent_rhs):
    lower_f = lower_panel[0]
    pivot_f = pivot_rhs[0]
    own_rows = lower_f.shape[1]
    block_count = lower_f.shape[2] // CB
    panel_number = lax.axis_index("panel")
    owner_block = panel_number * own_rows // CB
    partial_sum = jnp.zeros((2, pivot_f.shape[1], own_rows), F32)
    blocks = []
    for block in range(block_count):
        first = block * CB
        residual = (pivot_f.astype(F32) - partial_sum).astype(BF16)
        block_term = complex_product(inverse_cols[0], residual, "ri,sr->si")
        block_term = jnp.where(owner_block == block, block_term, 0.0)
        block_value = lax.psum(block_term.astype(BF16), "panel")
        blocks.append(block_value)
        partial_sum = partial_sum + complex_product(lower_f[:, :, first : first + CB], block_value, "rc,sc->sr")
    solution_f = jnp.concatenate(blocks, axis=2)
    own_solution = lax.dynamic_slice_in_dim(solution_f, panel_number * own_rows, own_rows, 2)
    applied = complex_product(update_panel[0], solution_f, "rc,sc->sr")
    child_update = (update_rhs[0].astype(F32) - applied).astype(BF16)
    parent_out = extend_add(child_update, row_maps, parent_rhs[0])
    return (own_solution[None], parent_out[None])


def solution(mesh):
    in_specs = (
        P("front", None, "panel", None),
        P("front", None, "panel", None),
        P("front", None, "panel", None),
        P("front", None, None, "panel"),
        P("front", None, None, "panel"),
        P(),
        P("front", None, None, "panel"),
    )
    out_specs = (P("front", None, None, "panel"), P("front", None, None, "panel"))

    def run(lower_panel, *others):
        blocks = lower_panel.shape[3] // CB
        one_block = mesh.shape["panel"] == blocks == len(SWAP)
        body = relay_body if one_block else summed_body
        call = jax.shard_map(body, mesh=mesh, in_specs=in_specs, out_specs=out_specs, check_vma=False)
        return call(lower_panel, *others)

    return run
```

```python
import functools

import jax
import jax.numpy as jnp
import numpy as np
from jax import lax
from jax.experimental import pallas as pl
from jax.experimental.pallas import tpu as pltpu
from jax.sharding import PartitionSpec as P

CB = 512
F32 = jnp.float32
BF16 = jnp.bfloat16

SWAP = ((0, 1), (1, 0), (2, 3), (3, 2), (4, 5), (5, 4), (6, 7), (7, 6))
CHAIN = (SWAP, ((1, 2),), SWAP, ((3, 4),), SWAP, ((5, 6),), SWAP)
RELAY = {
    2: {4: (0, 1), 6: (0, 2)},
    4: {6: (2, 2), 7: (1, 3)},
    6: {0: (4, 4), 2: (4, 3)},
}
OWN, PREV = "own", "prev"
SPREAD = (
    ((OWN, ((0, 2),)), (OWN, ((0, 4),)), (OWN, ((0, 6),))),
    ((OWN, ((1, 3),)), ((0, 0), ((2, 3),)), (OWN, ((1, 5),)), (OWN, ((1, 7),))),
    ((PREV, ((2, 4),)), (OWN, ((2, 4),)), (OWN, ((2, 6),))),
    ((OWN, ((3, 5),)), ((2, 1), ((4, 5),))),
    (
        (PREV, ((4, 6),)),
        (OWN, ((4, 6),)),
        (OWN, ((2, 0), (3, 1))),
        (OWN, ((4, 2),)),
        (OWN, ((4, 0),)),
        ((3, 0), ((5, 7),)),
    ),
    ((OWN, ((5, 7),)), ((4, 1), ((6, 7),)), ((4, 2), ((0, 1), (1, 0)))),
    ((OWN, ((6, 4), (5, 3))), (OWN, ((6, 2), (5, 1))), (OWN, ((6, 0),))),
    ((OWN, ((7, 5),)), (OWN, ((7, 3),)), (OWN, ((7, 1),))),
)


def spread_plan(count):
    have = [{p} for p in range(count)]

    def taken(edges, block_of):
        row = [-1] * count
        for source, dest in edges:
            block = block_of(source)
            if block is not None and block not in have[dest]:
                row[dest] = block
        return row

    def keep(row):
        for p, block in enumerate(row):
            if block >= 0:
                assert block not in have[p]
                have[p].add(block)

    chain = []
    spread = []
    for hop in range(count):
        if hop < len(CHAIN):

            def passed(p, hop=hop):
                if p in RELAY.get(hop, {}):
                    earlier, i = RELAY[hop][p]
                    return spread[earlier][i][p]
                return p if p <= hop else None

            row = taken(CHAIN[hop], passed)
            assert row[hop + 1] == hop
            keep(row)
            chain.append(row)
        rows = []
        for value, edges in SPREAD[hop]:
            if value == OWN:
                row = taken(edges, lambda source: source)
            elif value == PREV:
                row = taken(edges, lambda source: source - 1)
            else:
                row = taken(edges, lambda source, value=value: spread[value[0]][value[1]][source])
            assert sum(block >= 0 for block in row) == len(edges)
            keep(row)
            rows.append(row)
        spread.append(rows)
    swaps = []
    for even, odd in ((count - 3, count - 2), (count - 1, None)):
        row = taken(SWAP, lambda source, even=even, odd=odd: even if source % 2 else odd)
        keep(row)
        swaps.append(row)
    assert all(held == set(range(count)) for held in have)
    for p in range(count):
        for hop, rows in enumerate(spread):
            for row in rows:
                assert row[p] < 0 or row[p] > p or hop + 1 < p
        for hop, row in enumerate(chain):
            assert row[p] < 0 or row[p] > p or hop + 1 < p or (hop + 1 == p and row[p] == hop)
    return spread, chain, swaps


def stacked(value):
    return jnp.concatenate([value[0], value[1]], axis=0)


def turned_of(value):
    half = value.shape[0] // 2
    return jnp.concatenate([-value[half:], value[:half]], axis=0)


def apply_rows(value, matrix_real, matrix_imag):
    dims = (((1,), (1,)), ((), ()))
    return lax.dot_general(value, matrix_real, dims, preferred_element_type=F32) + lax.dot_general(
        turned_of(value), matrix_imag, dims, preferred_element_type=F32
    )


def apply_columns(value, matrix_real, matrix_imag):
    return jnp.dot(value, matrix_real, preferred_element_type=F32) + jnp.dot(
        turned_of(value), matrix_imag, preferred_element_type=F32
    )


def setup_kernel(place_ref, lower_ref, inverse_ref, pivot_ref, near_ref, inv_ref, rhs_ref, acc_l_ref, acc_u_ref, mine_ref, before_ref, sems):
    width = near_ref.shape[-1]
    block = jnp.maximum(place_ref[0] - 1, 0)
    columns = pl.ds(pl.multiple_of(block * width, width), width)
    copies = (
        pltpu.make_async_copy(pivot_ref.at[0], rhs_ref, sems.at[0]),
        pltpu.make_async_copy(inverse_ref.at[0], inv_ref, sems.at[1]),
        pltpu.make_async_copy(lower_ref.at[0, :, :, columns], near_ref, sems.at[2]),
    )
    for copy in copies:
        copy.start()
    for ref in (acc_l_ref, acc_u_ref, mine_ref, before_ref):
        ref[...] = jnp.zeros_like(ref)
    for copy in copies:
        copy.wait()


def setup(place, lower, inverse, pivot):
    rows = lower.shape[2]
    shots = pivot.shape[2]
    hbm = pl.BlockSpec(memory_space=pltpu.HBM)
    vmem = pl.BlockSpec(memory_space=pltpu.VMEM)
    weight = pltpu.VMEM((2, rows, CB), BF16)
    block = pltpu.VMEM((2, shots, CB), BF16)
    acc = pltpu.VMEM((2, shots, rows), F32)
    return pl.pallas_call(
        setup_kernel,
        out_shape=(weight, weight, block, acc, acc, block, block),
        in_specs=[pl.BlockSpec(memory_space=pltpu.SMEM), hbm, hbm, hbm],
        out_specs=(vmem,) * 7,
        scratch_shapes=[pltpu.SemaphoreType.DMA((3,))],
        compiler_params=pltpu.CompilerParams(vmem_limit_bytes=46 * 2**20),
        name="setup",
    )(place, lower, inverse, pivot)


def solve_kernel(hop, relays, place_ref, settled_ref, rhs_ref, acc_ref, near_ref, inv_ref, urgent_ref, mine_in, before_in, *refs):
    del settled_ref
    relay_refs, (out_ref, mine_ref, before_ref) = refs[: len(relays)], refs[len(relays) :]
    place = place_ref[0]
    shots = out_ref.shape[1]

    @pl.when(place != hop)
    def _():
        out_ref[...] = mine_in[...]
        mine_ref[...] = mine_in[...]
        before_ref[...] = before_in[...]

    for p, relay_ref in zip(relays, relay_refs):

        @pl.when(place == p)
        def _(relay_ref=relay_ref):
            out_ref[...] = relay_ref[...]

    @pl.when(place == hop)
    def _():
        residual = stacked(rhs_ref[...]).astype(F32)
        if hop > 0:
            residual = residual - stacked(acc_ref[...])
            residual = residual - apply_rows(stacked(urgent_ref[...]), near_ref[0], near_ref[1])
        term = apply_columns(residual.astype(BF16), inv_ref[0], inv_ref[1]).astype(BF16)
        for ref in (out_ref, mine_ref):
            ref[0] = term[:shots]
            ref[1] = term[shots:]
        before_ref[...] = urgent_ref[...]


def solve(hop, place, settled, rhs, acc, near, inv, urgent, mine, before, relays):
    vmem = pl.BlockSpec(memory_space=pltpu.VMEM)
    smem = pl.BlockSpec(memory_space=pltpu.SMEM)
    block = pltpu.VMEM(mine.shape, BF16)
    args = [rhs, acc, near, inv, urgent, mine, before, *relays.values()]
    return pl.pallas_call(
        functools.partial(solve_kernel, hop, tuple(relays)),
        out_shape=(block,) * 3,
        in_specs=[smem, pl.BlockSpec(memory_space=pl.ANY)] + [vmem] * len(args),
        out_specs=(vmem,) * 3,
        compiler_params=pltpu.CompilerParams(vmem_limit_bytes=16 * 2**20),
        name=f"solve_{hop}",
    )(place, settled, *args)


def gather_kernel(arrivals, left, place_ref, *refs):
    count = len(arrivals)
    parts = refs[:count]
    panel_ref, acc_in, acc_ref, buf, sems = refs[count:]
    width = buf.shape[-1]
    shots = acc_ref.shape[1]
    place = place_ref[0]
    blocks = []
    for row in arrivals:
        block = jnp.int32(-1)
        for p, value in enumerate(row):
            if value >= 0 and (value < p or not left):
                block = jnp.where(place == p, value, block)
        blocks.append(block)

    def copy_of(i):
        columns = pl.ds(pl.multiple_of(jnp.maximum(blocks[i], 0) * width, width), width)
        return pltpu.make_async_copy(panel_ref.at[0, :, :, columns], buf.at[i], sems.at[i])

    for i in range(count):

        @pl.when(blocks[i] >= 0)
        def _(i=i):
            copy_of(i).start()

    acc_ref[...] = acc_in[...]
    for i in range(count):

        @pl.when(blocks[i] >= 0)
        def _(i=i):
            copy_of(i).wait()
            product = apply_rows(stacked(parts[i][...]), buf[i, 0], buf[i, 1])
            acc_ref[0] += product[:shots]
            acc_ref[1] += product[shots:]


def pick_kernel(places, place_ref, *refs):
    out_ref = refs[-1]

    for p, ref in zip(places, refs):

        @pl.when(place_ref[0] == p)
        def _(ref=ref):
            out_ref[...] = ref[...]


def pick(name, place, values, default):
    count = lax.axis_size("panel")
    vmem = pl.BlockSpec(memory_space=pltpu.VMEM)
    args = [values.get(p, default) for p in range(count)]
    return pl.pallas_call(
        functools.partial(pick_kernel, tuple(range(count))),
        out_shape=pltpu.VMEM(default.shape, default.dtype),
        in_specs=[pl.BlockSpec(memory_space=pltpu.SMEM)] + [vmem] * count,
        out_specs=vmem,
        compiler_params=pltpu.CompilerParams(vmem_limit_bytes=16 * 2**20),
        name=name,
    )(place, *args)


def accumulate(name, left, place, items, panel, acc):
    items = [item for item in items if not left or any(0 <= block < p for p, block in enumerate(item[1]))]
    if not items:
        return acc
    parts = [item[0] for item in items]
    count = len(parts)
    vmem = pl.BlockSpec(memory_space=pltpu.VMEM)
    hbm = pl.BlockSpec(memory_space=pltpu.HBM)
    return pl.pallas_call(
        functools.partial(gather_kernel, [item[1] for item in items], left),
        out_shape=pltpu.VMEM(acc.shape, F32),
        in_specs=[pl.BlockSpec(memory_space=pltpu.SMEM)] + [vmem] * count + [hbm, vmem],
        out_specs=vmem,
        scratch_shapes=[pltpu.VMEM((count, 2, panel.shape[2], CB), BF16), pltpu.SemaphoreType.DMA((count,))],
        input_output_aliases={count + 2: 0} if left else {},
        compiler_params=pltpu.CompilerParams(vmem_limit_bytes=46 * 2**20),
        name=name,
    )(place, *parts, panel, acc)


def place_kernel(own_ref, other_ref, own_hot_ref, other_hot_ref, *out_refs):
    own = stacked(own_ref[...])
    other = stacked(other_ref[...])
    shots = own_ref.shape[1]
    for i, out_ref in enumerate(out_refs):
        rows = jnp.dot(own, own_hot_ref[i], preferred_element_type=F32) + jnp.dot(
            other, other_hot_ref[i], preferred_element_type=F32
        )
        rows = rows.astype(BF16)
        out_ref[0] = rows[:shots]
        out_ref[1] = rows[shots:]


def place_rows(own, other, own_hot, other_hot):
    vmem = pl.BlockSpec(memory_space=pltpu.VMEM)
    shape = jax.ShapeDtypeStruct(own.shape, BF16)
    count = own_hot.shape[0]
    return pl.pallas_call(
        place_kernel,
        out_shape=(shape,) * count,
        in_specs=[vmem] * 4,
        out_specs=(vmem,) * count,
        compiler_params=pltpu.CompilerParams(vmem_limit_bytes=24 * 2**20),
        name="place_rows",
    )(own, other, own_hot, other_hot)


def placements(row_maps, place, count, rows):
    own_map = lax.dynamic_index_in_dim(row_maps, lax.axis_index("front"), 0, keepdims=False)
    level = place // 2
    firsts = [place * rows, (count + place) * rows]
    for step in range(1, count // 2):
        far = level ^ step
        target = 2 * far + place % 2
        firsts.append(jnp.where(far < level, count + target, target) * rows)
    firsts = jnp.stack(firsts)
    targets = firsts[:, None] + jnp.arange(rows, dtype=jnp.int32)[None, :]

    def hot(device):
        mapped = lax.dynamic_slice_in_dim(own_map, device * rows, rows, 0)
        return (mapped[None, :, None] == targets[:, None, :]).astype(BF16)

    return hot(place), hot(place ^ 1)


def relay_body(lower_panel, inverse_cols, update_panel, pivot_rhs, update_rhs, row_maps, parent_rhs):
    shots = pivot_rhs.shape[2]
    upd_rows = update_panel.shape[2]
    count = lax.axis_size("panel")
    place = lax.axis_index("panel").astype(jnp.int32)
    level = place // 2
    spread_rows, chain_rows, swap_rows = spread_plan(count)

    def send(value, edges):
        return lax.ppermute(value, "panel", edges)

    place_ref = jnp.reshape(place, (1,))
    own_hot, other_hot = placements(row_maps, place, count, upd_rows)
    near, inv, rhs, acc_l, acc_u, mine, before = setup(place_ref, lower_panel, inverse_cols, pivot_rhs)
    urgent = mine
    came = []
    settled = [acc_u, acc_u]
    for hop in range(count):
        relays = {p: came[earlier][i] for p, (earlier, i) in RELAY.get(hop, {}).items()}
        passed, mine, before = solve(hop, place_ref, settled[hop], rhs, acc_l, near, inv, urgent, mine, before, relays)
        parts = [(mine, [hop if p == hop else -1 for p in range(count)])]
        if hop:
            parts.append((urgent, chain_rows[hop - 1]))
            parts += zip(came[hop - 1], spread_rows[hop - 1])
        if hop < len(CHAIN):
            urgent = send(passed, CHAIN[hop])
        came.append([])
        for value, edges in SPREAD[hop]:
            if value not in (OWN, PREV):
                value = came[value[0]][value[1]]
            else:
                value = mine if value == OWN else before
            came[hop].append(send(value, edges))
        if hop + 1 < count:
            acc_l = accumulate(f"lower_{hop}", True, place_ref, parts, lower_panel, acc_l)
        acc_u = accumulate(f"update_{hop}", False, place_ref, parts, update_panel, acc_u)
        settled.append(acc_u)

    def cross(name, blocks):
        values = {}
        for earlier, rows in enumerate(spread_rows):
            for i, row in enumerate(rows):
                for p in range(count):
                    if row[p] == blocks[p % 2]:
                        values[p] = came[earlier][i]
        return send(pick(name, place_ref, values, mine), SWAP)

    first = cross("pick_first", (count - 2, count - 3))
    second = cross("pick_second", (None, count - 1))
    parts = [(came[-1][i], row) for i, row in enumerate(spread_rows[-1])]
    parts.append((first, swap_rows[0]))
    acc_u = accumulate("update_late", False, place_ref, parts, update_panel, acc_u)
    parts = [(second, swap_rows[1])]
    acc_u = accumulate("update_last", False, place_ref, parts, update_panel, acc_u)
    child = (update_rhs[0].astype(F32) - acc_u).astype(BF16)
    other = send(child, SWAP)
    placed = place_rows(child, other, own_hot, other_hot)
    sums = [placed[0].astype(F32), placed[1].astype(F32)]
    for step in range(1, count // 2):
        moved = send(placed[1 + step], [(p, p ^ (2 * step)) for p in range(count)]).astype(F32)
        below = (level ^ step) < level
        sums[0] = sums[0] + jnp.where(below, moved, 0.0)
        sums[1] = sums[1] + jnp.where(below, 0.0, moved)
    odd_front = lax.axis_index("front") % 2 == 1
    kept = jnp.where(odd_front, sums[1], sums[0])
    given = jnp.where(odd_front, sums[0], sums[1]).astype(BF16)
    sibling = lax.ppermute(given, "front", [(f, f ^ 1) for f in range(lax.axis_size("front"))])
    parent_out = parent_rhs[0] + kept + sibling.astype(F32)
    return (mine[None], parent_out[None])


def select_rows(block_rows, index_map, base, owned):
    targets = base + jnp.arange(owned, dtype=jnp.int32)
    placement = (index_map[:, None] == targets[None, :]).astype(BF16)
    return jnp.einsum("csu,ur->csr", block_rows, placement, preferred_element_type=F32)


def extend_add(child_update, row_maps, parent_f):
    upd_rows = child_update.shape[2]
    panel_count = lax.axis_size("panel")
    panel_number = lax.axis_index("panel")
    front_number = lax.axis_index("front")
    parity = front_number % 2
    sibling_front = front_number + 1 - 2 * parity
    my_base = (parity * panel_count + panel_number) * upd_rows
    own_map = lax.dynamic_index_in_dim(row_maps, front_number, 0, keepdims=False)
    sibling_map = lax.dynamic_index_in_dim(row_maps, sibling_front, 0, keepdims=False)
    gathered = lax.all_gather(child_update, "panel", axis=2, tiled=True)
    pairs = [(source, source ^ 1) for source in range(lax.axis_size("front"))]
    sibling = lax.ppermute(gathered, "front", pairs)
    assembled = select_rows(gathered, own_map, my_base, upd_rows) + select_rows(
        sibling, sibling_map, my_base, upd_rows
    )
    return parent_f + assembled


def complex_product(matrix, vector, pattern):
    real_part = jnp.einsum(pattern, matrix[0], vector[0], preferred_element_type=F32) - jnp.einsum(
        pattern, matrix[1], vector[1], preferred_element_type=F32
    )
    imag_part = jnp.einsum(pattern, matrix[0], vector[1], preferred_element_type=F32) + jnp.einsum(
        pattern, matrix[1], vector[0], preferred_element_type=F32
    )
    return jnp.stack([real_part, imag_part])


def summed_body(lower_panel, inverse_cols, update_panel, pivot_rhs, update_rhs, row_maps, parent_rhs):
    lower_f = lower_panel[0]
    pivot_f = pivot_rhs[0]
    own_rows = lower_f.shape[1]
    block_count = lower_f.shape[2] // CB
    panel_number = lax.axis_index("panel")
    owner_block = panel_number * own_rows // CB
    partial_sum = jnp.zeros((2, pivot_f.shape[1], own_rows), F32)
    blocks = []
    for block in range(block_count):
        first = block * CB
        residual = (pivot_f.astype(F32) - partial_sum).astype(BF16)
        block_term = complex_product(inverse_cols[0], residual, "ri,sr->si")
        block_term = jnp.where(owner_block == block, block_term, 0.0)
        block_value = lax.psum(block_term.astype(BF16), "panel")
        blocks.append(block_value)
        partial_sum = partial_sum + complex_product(lower_f[:, :, first : first + CB], block_value, "rc,sc->sr")
    solution_f = jnp.concatenate(blocks, axis=2)
    own_solution = lax.dynamic_slice_in_dim(solution_f, panel_number * own_rows, own_rows, 2)
    applied = complex_product(update_panel[0], solution_f, "rc,sc->sr")
    child_update = (update_rhs[0].astype(F32) - applied).astype(BF16)
    parent_out = extend_add(child_update, row_maps, parent_rhs[0])
    return (own_solution[None], parent_out[None])


def solution(mesh):
    in_specs = (
        P("front", None, "panel", None),
        P("front", None, "panel", None),
        P("front", None, "panel", None),
        P("front", None, None, "panel"),
        P("front", None, None, "panel"),
        P(),
        P("front", None, None, "panel"),
    )
    out_specs = (P("front", None, None, "panel"), P("front", None, None, "panel"))

    def run(lower_panel, *others):
        blocks = lower_panel.shape[3] // CB
        one_block = mesh.shape["panel"] == blocks == len(SWAP)
        body = relay_body if one_block else summed_body
        call = jax.shard_map(body, mesh=mesh, in_specs=in_specs, out_specs=out_specs, check_vma=False)
        return call(lower_panel, *others)

    return run
```

```python
import functools

import jax
import jax.numpy as jnp
import numpy as np
from jax import lax
from jax.experimental import pallas as pl
from jax.experimental.pallas import tpu as pltpu
from jax.sharding import PartitionSpec as P

CB = 512
F32 = jnp.float32
BF16 = jnp.bfloat16

SWAP = ((0, 1), (1, 0), (2, 3), (3, 2), (4, 5), (5, 4), (6, 7), (7, 6))
CHAIN = (
    SWAP,
    ((1, 2), (2, 3), (3, 0), (0, 1), (4, 5), (5, 4), (6, 7), (7, 6)),
    SWAP,
    ((3, 4), (4, 5), (5, 2), (2, 3), (0, 1), (1, 0), (6, 7), (7, 6)),
    SWAP,
    ((5, 6), (6, 7), (7, 4), (4, 5), (0, 1), (1, 0), (2, 3), (3, 2)),
    SWAP,
)
RELAY = {
    2: {4: (0, 1), 6: (0, 0)},
    4: {7: (1, 0)},
    6: {0: (5, 4), 2: (5, 3)},
}
OWN, PREV = "own", "prev"
SPREAD = (
    ((OWN, ((0, 6),), 1), (OWN, ((0, 4),), 1), (OWN, ((0, 2),), 1)),
    ((OWN, ((1, 7),), 2), (OWN, ((1, 5),), 2), ((0, 2), ((2, 3),), 2), (OWN, ((1, 3),), 2)),
    ((PREV, ((2, 4),), 3), (OWN, ((2, 4),), 3)),
    ((OWN, ((3, 5), (2, 6)), 4), ((2, 1), ((4, 5),), 4)),
    ((PREV, ((4, 6),), 5), (OWN, ((4, 6),), 5), (OWN, ((2, 0), (3, 1)), 5), ((3, 0), ((5, 7),), 5)),
    (
        (OWN, ((5, 7),), 6),
        ((4, 1), ((6, 7),), 6),
        ((3, 0), ((6, 7),), 6),
        (OWN, ((5, 3), (4, 2)), 6),
        (OWN, ((5, 1), (4, 0)), 6),
        ((4, 2), ((0, 1), (1, 0)), 6),
    ),
    ((OWN, ((6, 4),), 7), (OWN, ((6, 2),), 7), (OWN, ((6, 0),), 7)),
    ((OWN, ((7, 5),), 8), (OWN, ((7, 3),), 8), (OWN, ((7, 1),), 8)),
)


def spread_plan(count):
    have = [{p} for p in range(count)]

    def taken(edges, block_of):
        row = [-1] * count
        for source, dest in edges:
            block = block_of(source)
            if block is not None and block not in have[dest]:
                row[dest] = block
        return row

    def keep(row):
        for p, block in enumerate(row):
            if block >= 0:
                assert block not in have[p]
                have[p].add(block)

    chain = []
    spread = []
    for hop in range(count):
        if hop < len(CHAIN):

            def passed(p, hop=hop):
                if p in RELAY.get(hop, {}):
                    earlier, i = RELAY[hop][p]
                    return spread[earlier][i][p]
                return p if p <= hop else None

            row = taken(CHAIN[hop], passed)
            assert row[hop + 1] == hop
            keep(row)
            chain.append(row)
        rows = []
        for value, edges, _ in SPREAD[hop]:
            if value == OWN:
                row = taken(edges, lambda source: source)
            elif value == PREV:
                row = taken(edges, lambda source: source - 1)
            else:
                row = taken(edges, lambda source, value=value: spread[value[0]][value[1]][source])
            assert sum(block >= 0 for block in row) == len(edges)
            keep(row)
            rows.append(row)
        spread.append(rows)
    swaps = []
    for even, odd in ((count - 3, count - 2), (count - 1, None)):
        row = taken(SWAP, lambda source, even=even, odd=odd: even if source % 2 else odd)
        keep(row)
        swaps.append(row)
    assert all(held == set(range(count)) for held in have)
    for p in range(count):
        for hop, rows in enumerate(spread):
            for (_, _, use), row in zip(SPREAD[hop], rows):
                assert use > hop and (row[p] < 0 or row[p] > p or use < p)
        for hop, row in enumerate(chain):
            assert row[p] < 0 or row[p] > p or hop + 1 < p or (hop + 1 == p and row[p] == hop)
    return spread, chain, swaps


def stacked(value):
    return jnp.concatenate([value[0], value[1]], axis=0)


def turned_of(value):
    half = value.shape[0] // 2
    return jnp.concatenate([-value[half:], value[:half]], axis=0)


def apply_rows(value, matrix_real, matrix_imag):
    dims = (((1,), (1,)), ((), ()))
    return lax.dot_general(value, matrix_real, dims, preferred_element_type=F32) + lax.dot_general(
        turned_of(value), matrix_imag, dims, preferred_element_type=F32
    )


def apply_columns(value, matrix_real, matrix_imag):
    return jnp.dot(value, matrix_real, preferred_element_type=F32) + jnp.dot(
        turned_of(value), matrix_imag, preferred_element_type=F32
    )


def setup_kernel(place_ref, lower_ref, near_ref, acc_l_ref, acc_u_ref, zero_ref, sem):
    width = near_ref.shape[-1]
    block = jnp.maximum(place_ref[0] - 1, 0)
    columns = pl.ds(pl.multiple_of(block * width, width), width)
    copy = pltpu.make_async_copy(lower_ref.at[0, :, :, columns], near_ref, sem)
    copy.start()
    for ref in (acc_l_ref, acc_u_ref, zero_ref):
        ref[...] = jnp.zeros_like(ref)
    copy.wait()


def setup(place, lower, shots):
    rows = lower.shape[2]
    vmem = pl.BlockSpec(memory_space=pltpu.VMEM)
    acc = pltpu.VMEM((2, shots, rows), F32)
    return pl.pallas_call(
        setup_kernel,
        out_shape=(pltpu.VMEM((2, rows, CB), BF16), acc, acc, pltpu.VMEM((2, shots, CB), BF16)),
        in_specs=[pl.BlockSpec(memory_space=pltpu.SMEM), pl.BlockSpec(memory_space=pltpu.HBM)],
        out_specs=(vmem,) * 4,
        scratch_shapes=[pltpu.SemaphoreType.DMA(())],
        compiler_params=pltpu.CompilerParams(vmem_limit_bytes=46 * 2**20),
        name="setup",
    )(place, lower)


def first_kernel(place_ref, rhs_ref, inv_ref, out_ref, mine_ref):
    shots = out_ref.shape[1]

    @pl.when(place_ref[0] != 0)
    def _():
        out_ref[...] = jnp.zeros_like(out_ref)
        mine_ref[...] = jnp.zeros_like(mine_ref)

    @pl.when(place_ref[0] == 0)
    def _():
        term = apply_columns(stacked(rhs_ref[0]), inv_ref[0, 0], inv_ref[0, 1]).astype(BF16)
        for ref in (out_ref, mine_ref):
            ref[0] = term[:shots]
            ref[1] = term[shots:]


def solve_first(place, rhs, inv):
    vmem = pl.BlockSpec(memory_space=pltpu.VMEM)
    return pl.pallas_call(
        first_kernel,
        out_shape=(pltpu.VMEM(rhs.shape[1:], BF16),) * 2,
        in_specs=[pl.BlockSpec(memory_space=pltpu.SMEM), vmem, vmem],
        out_specs=(vmem,) * 2,
        compiler_params=pltpu.CompilerParams(vmem_limit_bytes=16 * 2**20),
        name="solve_0",
    )(place, rhs, inv)


def solve_kernel(hop, relays, settled, place_ref, *refs):
    rhs_ref, acc_ref, near_ref, inv_ref, urgent_ref, mine_in, before_in, *refs = refs[settled:]
    relay_refs, (out_ref, mine_ref, before_ref) = refs[: len(relays)], refs[len(relays) :]
    place = place_ref[0]
    shots = out_ref.shape[1]

    @pl.when(place != hop)
    def _():
        out_ref[...] = mine_in[...]
        mine_ref[...] = mine_in[...]
        before_ref[...] = before_in[...]

    for p, relay_ref in zip(relays, relay_refs):

        @pl.when(place == p)
        def _(relay_ref=relay_ref):
            out_ref[...] = relay_ref[...]

    @pl.when(place == hop)
    def _():
        residual = stacked(rhs_ref[0]).astype(F32) - stacked(acc_ref[...])
        residual = residual - apply_rows(stacked(urgent_ref[...]), near_ref[0], near_ref[1])
        term = apply_columns(residual.astype(BF16), inv_ref[0, 0], inv_ref[0, 1]).astype(BF16)
        for ref in (out_ref, mine_ref):
            ref[0] = term[:shots]
            ref[1] = term[shots:]
        before_ref[...] = urgent_ref[...]


def solve(hop, place, settled, rhs, acc, near, inv, urgent, mine, before, relays):
    vmem = pl.BlockSpec(memory_space=pltpu.VMEM)
    smem = pl.BlockSpec(memory_space=pltpu.SMEM)
    block = pltpu.VMEM(mine.shape, BF16)
    args = [rhs, acc, near, inv, urgent, mine, before, *relays.values()]
    return pl.pallas_call(
        functools.partial(solve_kernel, hop, tuple(relays), len(settled)),
        out_shape=(block,) * 3,
        in_specs=[smem] + [pl.BlockSpec(memory_space=pl.ANY)] * len(settled) + [vmem] * len(args),
        out_specs=(vmem,) * 3,
        compiler_params=pltpu.CompilerParams(vmem_limit_bytes=16 * 2**20),
        name=f"solve_{hop}",
    )(place, *settled, *args)


def gather_kernel(arrivals, left, final, place_ref, *refs):
    count = len(arrivals)
    parts = refs[:count]
    refs = refs[count:]
    if final:
        panel_ref, acc_in, rhs_ref, out_ref, buf, sems, acc_ref = refs
    else:
        panel_ref, acc_in, acc_ref, buf, sems = refs
    width = buf.shape[-1]
    shots = acc_ref.shape[1]
    place = place_ref[0]
    blocks = []
    for row in arrivals:
        block = jnp.int32(-1)
        for p, value in enumerate(row):
            if value >= 0 and (value < p or not left):
                block = jnp.where(place == p, value, block)
        blocks.append(block)

    def copy_of(i):
        columns = pl.ds(pl.multiple_of(jnp.maximum(blocks[i], 0) * width, width), width)
        return pltpu.make_async_copy(panel_ref.at[0, :, :, columns], buf.at[i], sems.at[i])

    for i in range(count):

        @pl.when(blocks[i] >= 0)
        def _(i=i):
            copy_of(i).start()

    acc_ref[...] = acc_in[...]
    for i in range(count):

        @pl.when(blocks[i] >= 0)
        def _(i=i):
            copy_of(i).wait()
            product = apply_rows(stacked(parts[i][...]), buf[i, 0], buf[i, 1])
            acc_ref[0] += product[:shots]
            acc_ref[1] += product[shots:]

    if final:
        out_ref[...] = (rhs_ref[0].astype(F32) - acc_ref[...]).astype(BF16)


def accumulate(name, left, place, items, panel, acc, rhs=None):
    items = [item for item in items if not left or any(0 <= block < p for p, block in enumerate(item[1]))]
    if not items:
        return acc
    parts = [item[0] for item in items]
    count = len(parts)
    final = rhs is not None
    vmem = pl.BlockSpec(memory_space=pltpu.VMEM)
    hbm = pl.BlockSpec(memory_space=pltpu.HBM)
    scratch = [pltpu.VMEM((count, 2, panel.shape[2], CB), BF16), pltpu.SemaphoreType.DMA((count,))]
    return pl.pallas_call(
        functools.partial(gather_kernel, [item[1] for item in items], left, final),
        out_shape=pltpu.VMEM(acc.shape, BF16 if final else F32),
        in_specs=[pl.BlockSpec(memory_space=pltpu.SMEM)] + [vmem] * count + [hbm, vmem] + [vmem] * final,
        out_specs=vmem,
        scratch_shapes=scratch + [pltpu.VMEM(acc.shape, F32)] * final,
        input_output_aliases={count + 2: 0} if left else {},
        compiler_params=pltpu.CompilerParams(vmem_limit_bytes=46 * 2**20),
        name=name,
    )(place, *parts, panel, acc, *([rhs] if final else []))


def pick_kernel(places, keep, place_ref, settled_ref, *refs):
    del settled_ref
    count = len(places)
    out_ref, sems = refs[count + 1], refs[-1]
    kept = pltpu.make_async_copy(refs[count], refs[count + 2].at[0], sems.at[1]) if keep else None
    if keep:
        kept.start()

    for p, ref in zip(places, refs):

        @pl.when(place_ref[0] == p)
        def _(ref=ref):
            copy = pltpu.make_async_copy(ref, out_ref, sems.at[0])
            copy.start()
            copy.wait()

    if keep:
        kept.wait()


def pick(name, place, settled, values, default, keep):
    count = lax.axis_size("panel")
    vmem = pl.BlockSpec(memory_space=pltpu.VMEM)
    anywhere = pl.BlockSpec(memory_space=pl.ANY)
    args = [values.get(p, default) for p in range(count)] + [default]
    out_shape = [pltpu.VMEM(default.shape, default.dtype)]
    if keep:
        out_shape.append(jax.ShapeDtypeStruct((1, *default.shape), default.dtype))
    return pl.pallas_call(
        functools.partial(pick_kernel, tuple(range(count)), keep),
        out_shape=out_shape,
        in_specs=[pl.BlockSpec(memory_space=pltpu.SMEM)] + [anywhere] * (1 + len(args)),
        out_specs=[vmem] + [anywhere] * keep,
        scratch_shapes=[pltpu.SemaphoreType.DMA((2,))],
        compiler_params=pltpu.CompilerParams(vmem_limit_bytes=16 * 2**20),
        name=name,
    )(place, settled, *args)


def place_kernel(own_ref, other_ref, own_hot_ref, other_hot_ref, *out_refs):
    own = stacked(own_ref[...])
    other = stacked(other_ref[...])
    shots = own_ref.shape[1]
    for i, out_ref in enumerate(out_refs):
        rows = jnp.dot(own, own_hot_ref[i], preferred_element_type=F32) + jnp.dot(
            other, other_hot_ref[i], preferred_element_type=F32
        )
        rows = rows.astype(BF16)
        out_ref[0] = rows[:shots]
        out_ref[1] = rows[shots:]


def place_rows(own, other, own_hot, other_hot):
    vmem = pl.BlockSpec(memory_space=pltpu.VMEM)
    shape = jax.ShapeDtypeStruct(own.shape, BF16)
    count = own_hot.shape[0]
    return pl.pallas_call(
        place_kernel,
        out_shape=(shape,) * count,
        in_specs=[vmem] * 4,
        out_specs=(vmem,) * count,
        compiler_params=pltpu.CompilerParams(vmem_limit_bytes=24 * 2**20),
        name="place_rows",
    )(own, other, own_hot, other_hot)


def placements(row_maps, place, count, rows):
    own_map = lax.dynamic_index_in_dim(row_maps, lax.axis_index("front"), 0, keepdims=False)
    level = place // 2
    firsts = [place * rows, (count + place) * rows]
    for step in range(1, count // 2):
        far = level ^ step
        target = 2 * far + place % 2
        firsts.append(jnp.where(far < level, count + target, target) * rows)
    firsts = jnp.stack(firsts)
    targets = firsts[:, None] + jnp.arange(rows, dtype=jnp.int32)[None, :]

    def hot(device):
        mapped = lax.dynamic_slice_in_dim(own_map, device * rows, rows, 0)
        return (mapped[None, :, None] == targets[:, None, :]).astype(BF16)

    return hot(place), hot(place ^ 1)


def relay_body(lower_panel, inverse_cols, update_panel, pivot_rhs, update_rhs, row_maps, parent_rhs):
    shots = pivot_rhs.shape[2]
    upd_rows = update_panel.shape[2]
    count = lax.axis_size("panel")
    place = lax.axis_index("panel").astype(jnp.int32)
    level = place // 2
    spread_rows, chain_rows, swap_rows = spread_plan(count)

    def send(value, edges):
        return lax.ppermute(value, "panel", edges)

    place_ref = jnp.reshape(place, (1,))
    own_hot, other_hot = placements(row_maps, place, count, upd_rows)
    near, acc_l, acc_u, before = setup(place_ref, lower_panel, shots)
    passed, mine = solve_first(place_ref, pivot_rhs, inverse_cols)
    urgent = None
    came = []
    settled = [acc_u, acc_u]
    for hop in range(count):
        relays = {p: came[earlier][i] for p, (earlier, i) in RELAY.get(hop, {}).items()}
        if hop:
            after = [settled[hop]]
            passed, mine, before = solve(
                hop, place_ref, after, pivot_rhs, acc_l, near, inverse_cols, urgent, mine, before, relays
            )
        parts = [(mine, [hop if p == hop else -1 for p in range(count)])]
        if hop:
            parts.append((urgent, chain_rows[hop - 1]))
        for earlier in range(hop):
            for i, (_, _, use) in enumerate(SPREAD[earlier]):
                if use == hop:
                    parts.append((came[earlier][i], spread_rows[earlier][i]))
        if hop < len(CHAIN):
            urgent = send(passed, CHAIN[hop])
        came.append([])
        for value, edges, _ in SPREAD[hop]:
            if value not in (OWN, PREV):
                value = came[value[0]][value[1]]
            else:
                value = mine if value == OWN else before
            came[hop].append(send(value, edges))
        if hop + 1 < count:
            acc_l = accumulate(f"lower_{hop}", True, place_ref, parts, lower_panel, acc_l)
        acc_u = accumulate(f"update_{hop}", False, place_ref, parts, update_panel, acc_u)
        settled.append(acc_u)

    def cross(name, settled, blocks, keep):
        values = {}
        for earlier, rows in enumerate(spread_rows):
            for i, row in enumerate(rows):
                for p in range(count):
                    if row[p] == blocks[p % 2]:
                        values[p] = came[earlier][i]
        value, *kept = pick(name, place_ref, settled, values, mine, keep)
        return (send(value, SWAP), *kept)

    first, solved = cross("pick_first", settled[count], (count - 2, count - 3), True)
    (second,) = cross("pick_second", settled[count + 1], (None, count - 1), False)
    parts = [(came[-1][i], row) for i, row in enumerate(spread_rows[-1])]
    parts.append((first, swap_rows[0]))
    acc_u = accumulate("update_late", False, place_ref, parts, update_panel, acc_u)
    parts = [(second, swap_rows[1])]
    child = accumulate("update_last", False, place_ref, parts, update_panel, acc_u, update_rhs)
    other = send(child, SWAP)
    placed = place_rows(child, other, own_hot, other_hot)
    sums = [placed[0].astype(F32), placed[1].astype(F32)]
    for step in range(1, count // 2):
        moved = send(placed[1 + step], [(p, p ^ (2 * step)) for p in range(count)]).astype(F32)
        below = (level ^ step) < level
        sums[0] = sums[0] + jnp.where(below, moved, 0.0)
        sums[1] = sums[1] + jnp.where(below, 0.0, moved)
    odd_front = lax.axis_index("front") % 2 == 1
    kept = jnp.where(odd_front, sums[1], sums[0])
    given = jnp.where(odd_front, sums[0], sums[1]).astype(BF16)
    sibling = lax.ppermute(given, "front", [(f, f ^ 1) for f in range(lax.axis_size("front"))])
    parent_out = parent_rhs[0] + kept + sibling.astype(F32)
    return (solved, parent_out[None])


def select_rows(block_rows, index_map, base, owned):
    targets = base + jnp.arange(owned, dtype=jnp.int32)
    placement = (index_map[:, None] == targets[None, :]).astype(BF16)
    return jnp.einsum("csu,ur->csr", block_rows, placement, preferred_element_type=F32)


def extend_add(child_update, row_maps, parent_f):
    upd_rows = child_update.shape[2]
    panel_count = lax.axis_size("panel")
    panel_number = lax.axis_index("panel")
    front_number = lax.axis_index("front")
    parity = front_number % 2
    sibling_front = front_number + 1 - 2 * parity
    my_base = (parity * panel_count + panel_number) * upd_rows
    own_map = lax.dynamic_index_in_dim(row_maps, front_number, 0, keepdims=False)
    sibling_map = lax.dynamic_index_in_dim(row_maps, sibling_front, 0, keepdims=False)
    gathered = lax.all_gather(child_update, "panel", axis=2, tiled=True)
    pairs = [(source, source ^ 1) for source in range(lax.axis_size("front"))]
    sibling = lax.ppermute(gathered, "front", pairs)
    assembled = select_rows(gathered, own_map, my_base, upd_rows) + select_rows(
        sibling, sibling_map, my_base, upd_rows
    )
    return parent_f + assembled


def complex_product(matrix, vector, pattern):
    real_part = jnp.einsum(pattern, matrix[0], vector[0], preferred_element_type=F32) - jnp.einsum(
        pattern, matrix[1], vector[1], preferred_element_type=F32
    )
    imag_part = jnp.einsum(pattern, matrix[0], vector[1], preferred_element_type=F32) + jnp.einsum(
        pattern, matrix[1], vector[0], preferred_element_type=F32
    )
    return jnp.stack([real_part, imag_part])


def summed_body(lower_panel, inverse_cols, update_panel, pivot_rhs, update_rhs, row_maps, parent_rhs):
    lower_f = lower_panel[0]
    pivot_f = pivot_rhs[0]
    own_rows = lower_f.shape[1]
    block_count = lower_f.shape[2] // CB
    panel_number = lax.axis_index("panel")
    owner_block = panel_number * own_rows // CB
    partial_sum = jnp.zeros((2, pivot_f.shape[1], own_rows), F32)
    blocks = []
    for block in range(block_count):
        first = block * CB
        residual = (pivot_f.astype(F32) - partial_sum).astype(BF16)
        block_term = complex_product(inverse_cols[0], residual, "ri,sr->si")
        block_term = jnp.where(owner_block == block, block_term, 0.0)
        block_value = lax.psum(block_term.astype(BF16), "panel")
        blocks.append(block_value)
        partial_sum = partial_sum + complex_product(lower_f[:, :, first : first + CB], block_value, "rc,sc->sr")
    solution_f = jnp.concatenate(blocks, axis=2)
    own_solution = lax.dynamic_slice_in_dim(solution_f, panel_number * own_rows, own_rows, 2)
    applied = complex_product(update_panel[0], solution_f, "rc,sc->sr")
    child_update = (update_rhs[0].astype(F32) - applied).astype(BF16)
    parent_out = extend_add(child_update, row_maps, parent_rhs[0])
    return (own_solution[None], parent_out[None])


def solution(mesh):
    in_specs = (
        P("front", None, "panel", None),
        P("front", None, "panel", None),
        P("front", None, "panel", None),
        P("front", None, None, "panel"),
        P("front", None, None, "panel"),
        P(),
        P("front", None, None, "panel"),
    )
    out_specs = (P("front", None, None, "panel"), P("front", None, None, "panel"))

    def run(lower_panel, *others):
        blocks = lower_panel.shape[3] // CB
        one_block = mesh.shape["panel"] == blocks == len(SWAP)
        body = relay_body if one_block else summed_body
        call = jax.shard_map(body, mesh=mesh, in_specs=in_specs, out_specs=out_specs, check_vma=False)
        return call(lower_panel, *others)

    return run
```

```python
import functools

import jax
import jax.numpy as jnp
import numpy as np
from jax import lax
from jax.experimental import pallas as pl
from jax.experimental.pallas import tpu as pltpu
from jax.sharding import PartitionSpec as P

CB = 512
F32 = jnp.float32
BF16 = jnp.bfloat16

SWAP = ((0, 1), (1, 0), (2, 3), (3, 2), (4, 5), (5, 4), (6, 7), (7, 6))
CHAIN = (
    SWAP,
    ((1, 2), (2, 3), (3, 0), (0, 1), (4, 5), (5, 4), (6, 7), (7, 6)),
    SWAP,
    ((3, 4), (4, 5), (5, 2), (2, 3), (0, 1), (1, 0), (6, 7), (7, 6)),
    SWAP,
    ((5, 6), (6, 7), (7, 4), (4, 5), (0, 1), (1, 0), (2, 3), (3, 2)),
    SWAP,
)
RELAY = {
    2: {4: (0, 1), 6: (0, 0)},
    4: {7: (1, 0)},
    6: {0: (5, 4), 2: (5, 3)},
}
OWN, PREV = "own", "prev"
SPREAD = (
    ((OWN, ((0, 6),), 1), (OWN, ((0, 4),), 1), (OWN, ((0, 2),), 1)),
    ((OWN, ((1, 7),), 2), (OWN, ((1, 5),), 2), ((0, 2), ((2, 3),), 2), (OWN, ((1, 3),), 2)),
    ((PREV, ((2, 4),), 3), (OWN, ((2, 4),), 3)),
    ((OWN, ((3, 5), (2, 6)), 4), ((2, 1), ((4, 5),), 4)),
    ((PREV, ((4, 6),), 5), (OWN, ((4, 6),), 5), (OWN, ((2, 0), (3, 1)), 5), ((3, 0), ((5, 7),), 5)),
    (
        (OWN, ((5, 7),), 6),
        ((4, 1), ((6, 7),), 6),
        ((3, 0), ((6, 7),), 6),
        (OWN, ((5, 3), (4, 2)), 6),
        (OWN, ((5, 1), (4, 0)), 6),
        ((4, 2), ((0, 1), (1, 0)), 6),
    ),
    ((OWN, ((6, 4),), 7), (OWN, ((6, 2),), 7), (OWN, ((6, 0),), 7)),
    ((OWN, ((7, 5),), 8), (OWN, ((7, 3),), 8), (OWN, ((7, 1),), 8)),
)


PARTS = 2


def spread_plan(count):
    have = [{p} for p in range(count)]

    def taken(edges, block_of):
        row = [-1] * count
        for source, dest in edges:
            block = block_of(source)
            if block is not None and block not in have[dest]:
                row[dest] = block
        return row

    def keep(row):
        for p, block in enumerate(row):
            if block >= 0:
                assert block not in have[p]
                have[p].add(block)

    chain = []
    spread = []
    for hop in range(count):
        if hop < len(CHAIN):

            def passed(p, hop=hop):
                if p in RELAY.get(hop, {}):
                    earlier, i = RELAY[hop][p]
                    return spread[earlier][i][p]
                return p if p <= hop else None

            row = taken(CHAIN[hop], passed)
            assert row[hop + 1] == hop
            keep(row)
            chain.append(row)
        rows = []
        for value, edges, _ in SPREAD[hop]:
            if value == OWN:
                row = taken(edges, lambda source: source)
            elif value == PREV:
                row = taken(edges, lambda source: source - 1)
            else:
                row = taken(edges, lambda source, value=value: spread[value[0]][value[1]][source])
            assert sum(block >= 0 for block in row) == len(edges)
            keep(row)
            rows.append(row)
        spread.append(rows)
    swaps = []
    for even, odd in ((count - 3, count - 2), (count - 1, None)):
        row = taken(SWAP, lambda source, even=even, odd=odd: even if source % 2 else odd)
        keep(row)
        swaps.append(row)
    assert all(held == set(range(count)) for held in have)
    for p in range(count):
        for hop, rows in enumerate(spread):
            for (_, _, use), row in zip(SPREAD[hop], rows):
                assert use > hop and (row[p] < 0 or row[p] > p or use < p)
        for hop, row in enumerate(chain):
            assert row[p] < 0 or row[p] > p or hop + 1 < p or (hop + 1 == p and row[p] == hop)
    return spread, chain, swaps


def stacked(value):
    return jnp.concatenate([value[0], value[1]], axis=0)


def turned_of(value):
    half = value.shape[0] // 2
    return jnp.concatenate([-value[half:], value[:half]], axis=0)


def apply_rows(value, matrix_real, matrix_imag):
    dims = (((1,), (1,)), ((), ()))
    return lax.dot_general(value, matrix_real, dims, preferred_element_type=F32) + lax.dot_general(
        turned_of(value), matrix_imag, dims, preferred_element_type=F32
    )


def apply_columns(value, matrix_real, matrix_imag):
    return jnp.dot(value, matrix_real, preferred_element_type=F32) + jnp.dot(
        turned_of(value), matrix_imag, preferred_element_type=F32
    )


def setup_kernel(place_ref, lower_ref, near_ref, acc_l_ref, acc_u_ref, zero_ref, sem):
    width = near_ref.shape[-1]
    block = jnp.maximum(place_ref[0] - 1, 0)
    columns = pl.ds(pl.multiple_of(block * width, width), width)
    copy = pltpu.make_async_copy(lower_ref.at[0, :, :, columns], near_ref, sem)
    copy.start()
    for ref in (acc_l_ref, acc_u_ref, zero_ref):
        ref[...] = jnp.zeros_like(ref)
    copy.wait()


def setup(place, lower, shots):
    rows = lower.shape[2]
    vmem = pl.BlockSpec(memory_space=pltpu.VMEM)
    acc = pltpu.VMEM((2, shots, rows), F32)
    return pl.pallas_call(
        setup_kernel,
        out_shape=(pltpu.VMEM((2, rows, CB), BF16), acc, acc, pltpu.VMEM((2, shots, CB), BF16)),
        in_specs=[pl.BlockSpec(memory_space=pltpu.SMEM), pl.BlockSpec(memory_space=pltpu.HBM)],
        out_specs=(vmem,) * 4,
        scratch_shapes=[pltpu.SemaphoreType.DMA(())],
        compiler_params=pltpu.CompilerParams(vmem_limit_bytes=46 * 2**20),
        name="setup",
    )(place, lower)


def first_kernel(place_ref, rhs_ref, inv_ref, out_ref, mine_ref):
    shots = out_ref.shape[1]

    @pl.when(place_ref[0] != 0)
    def _():
        out_ref[...] = jnp.zeros_like(out_ref)
        mine_ref[...] = jnp.zeros_like(mine_ref)

    @pl.when(place_ref[0] == 0)
    def _():
        term = apply_columns(stacked(rhs_ref[0]), inv_ref[0, 0], inv_ref[0, 1]).astype(BF16)
        for ref in (out_ref, mine_ref):
            ref[0] = term[:shots]
            ref[1] = term[shots:]


def solve_first(place, rhs, inv):
    vmem = pl.BlockSpec(memory_space=pltpu.VMEM)
    return pl.pallas_call(
        first_kernel,
        out_shape=(pltpu.VMEM(rhs.shape[1:], BF16),) * 2,
        in_specs=[pl.BlockSpec(memory_space=pltpu.SMEM), vmem, vmem],
        out_specs=(vmem,) * 2,
        compiler_params=pltpu.CompilerParams(vmem_limit_bytes=16 * 2**20),
        name="solve_0",
    )(place, rhs, inv)


def solve_kernel(hop, relays, settled, place_ref, *refs):
    rhs_ref, acc_ref, near_ref, inv_ref, urgent_ref, mine_in, before_in, *refs = refs[settled:]
    relay_refs, (out_ref, mine_ref, before_ref) = refs[: len(relays)], refs[len(relays) :]
    place = place_ref[0]
    shots = out_ref.shape[1]

    @pl.when(place != hop)
    def _():
        out_ref[...] = mine_in[...]
        mine_ref[...] = mine_in[...]
        before_ref[...] = before_in[...]

    for p, relay_ref in zip(relays, relay_refs):

        @pl.when(place == p)
        def _(relay_ref=relay_ref):
            out_ref[...] = relay_ref[...]

    @pl.when(place == hop)
    def _():
        residual = stacked(rhs_ref[0]).astype(F32) - stacked(acc_ref[...])
        residual = residual - apply_rows(stacked(urgent_ref[...]), near_ref[0], near_ref[1])
        term = apply_columns(residual.astype(BF16), inv_ref[0, 0], inv_ref[0, 1]).astype(BF16)
        for ref in (out_ref, mine_ref):
            ref[0] = term[:shots]
            ref[1] = term[shots:]
        before_ref[...] = urgent_ref[...]


def solve(hop, place, settled, rhs, acc, near, inv, urgent, mine, before, relays):
    vmem = pl.BlockSpec(memory_space=pltpu.VMEM)
    smem = pl.BlockSpec(memory_space=pltpu.SMEM)
    block = pltpu.VMEM(mine.shape, BF16)
    args = [rhs, acc, near, inv, urgent, mine, before, *relays.values()]
    return pl.pallas_call(
        functools.partial(solve_kernel, hop, tuple(relays), len(settled)),
        out_shape=(block,) * 3,
        in_specs=[smem] + [pl.BlockSpec(memory_space=pl.ANY)] * len(settled) + [vmem] * len(args),
        out_specs=(vmem,) * 3,
        compiler_params=pltpu.CompilerParams(vmem_limit_bytes=16 * 2**20),
        name=f"solve_{hop}",
    )(place, *settled, *args)


def gather_kernel(arrivals, left, part, place_ref, *refs):
    count = len(arrivals)
    parts = refs[:count]
    refs = refs[count:]
    final = part is not None
    if final:
        panel_ref, acc_in, rhs_ref, out_ref, buf, sems, acc_ref = refs
    else:
        panel_ref, acc_in, acc_ref, buf, sems = refs
    width = buf.shape[-1]
    shots = acc_ref.shape[1]
    place = place_ref[0]
    blocks = []
    for row in arrivals:
        block = jnp.int32(-1)
        for p, value in enumerate(row):
            if value >= 0 and (value < p or not left):
                block = jnp.where(place == p, value, block)
        blocks.append(block)

    def copy_of(i):
        columns = pl.ds(pl.multiple_of(jnp.maximum(blocks[i], 0) * width, width), width)
        return pltpu.make_async_copy(panel_ref.at[0, :, :, columns], buf.at[i], sems.at[i])

    for i in range(count):

        @pl.when(blocks[i] >= 0)
        def _(i=i):
            copy_of(i).start()

    rows = slice(part * shots, (part + 1) * shots) if final else slice(None)
    acc_ref[...] = acc_in[:, rows]
    for i in range(count):

        @pl.when(blocks[i] >= 0)
        def _(i=i):
            copy_of(i).wait()
            product = apply_rows(stacked(parts[i][...]), buf[i, 0], buf[i, 1])
            acc_ref[0] += product[:shots]
            acc_ref[1] += product[shots:]

    if final:
        out_ref[...] = (rhs_ref[0, :, rows].astype(F32) - acc_ref[...]).astype(BF16)


def accumulate(name, left, place, items, panel, acc, rhs=None, part=None):
    items = [item for item in items if not left or any(0 <= block < p for p, block in enumerate(item[1]))]
    if not items:
        return acc
    parts = [item[0] for item in items]
    count = len(parts)
    final = part is not None
    shape = (2, acc.shape[1] // PARTS, acc.shape[2]) if final else acc.shape
    vmem = pl.BlockSpec(memory_space=pltpu.VMEM)
    hbm = pl.BlockSpec(memory_space=pltpu.HBM)
    scratch = [pltpu.VMEM((count, 2, panel.shape[2], CB), BF16), pltpu.SemaphoreType.DMA((count,))]
    return pl.pallas_call(
        functools.partial(gather_kernel, [item[1] for item in items], left, part),
        out_shape=pltpu.VMEM(shape, BF16 if final else F32),
        in_specs=[pl.BlockSpec(memory_space=pltpu.SMEM)] + [vmem] * count + [hbm, vmem] + [vmem] * final,
        out_specs=vmem,
        scratch_shapes=scratch + [pltpu.VMEM(shape, F32)] * final,
        input_output_aliases={count + 2: 0} if left else {},
        compiler_params=pltpu.CompilerParams(vmem_limit_bytes=46 * 2**20),
        name=name,
    )(place, *parts, panel, acc, *([rhs] if final else []))


def pick_kernel(places, keep, place_ref, settled_ref, *refs):
    del settled_ref
    count = len(places)
    sems = refs[-1]
    out_refs = refs[count + 1 : -1]
    if keep:
        out_refs, kept_ref = out_refs[:-1], out_refs[-1]
        kept = pltpu.make_async_copy(refs[count], kept_ref.at[0], sems.at[len(out_refs)])
        kept.start()
    size = out_refs[0].shape[1]

    for p, ref in zip(places, refs):

        @pl.when(place_ref[0] == p)
        def _(ref=ref):
            copies = [
                pltpu.make_async_copy(ref.at[:, pl.ds(i * size, size)], out_ref, sems.at[i])
                for i, out_ref in enumerate(out_refs)
            ]
            for copy in copies:
                copy.start()
            for copy in copies:
                copy.wait()

    if keep:
        kept.wait()


def pick(name, place, settled, values, default, keep, cuts):
    count = lax.axis_size("panel")
    vmem = pl.BlockSpec(memory_space=pltpu.VMEM)
    anywhere = pl.BlockSpec(memory_space=pl.ANY)
    args = [values.get(p, default) for p in range(count)] + [default]
    shots = default.shape[1]
    out_shape = [pltpu.VMEM((2, shots // cuts, CB), default.dtype)] * cuts
    if keep:
        out_shape.append(jax.ShapeDtypeStruct((1, *default.shape), default.dtype))
    return pl.pallas_call(
        functools.partial(pick_kernel, tuple(range(count)), keep),
        out_shape=out_shape,
        in_specs=[pl.BlockSpec(memory_space=pltpu.SMEM)] + [anywhere] * (1 + len(args)),
        out_specs=[vmem] * cuts + [anywhere] * keep,
        scratch_shapes=[pltpu.SemaphoreType.DMA((cuts + 1,))],
        compiler_params=pltpu.CompilerParams(vmem_limit_bytes=16 * 2**20),
        name=name,
    )(place, settled, *args)


def place_kernel(cuts, *refs):
    own_refs, other_refs = refs[:cuts], refs[cuts : 2 * cuts]
    own_hot_ref, other_hot_ref = refs[2 * cuts : 2 * cuts + 2]
    out_refs = refs[2 * cuts + 2 :]
    size = own_refs[0].shape[1]
    for cut in range(cuts):
        own = stacked(own_refs[cut][...])
        other = stacked(other_refs[cut][...])
        for i, out_ref in enumerate(out_refs):
            rows = jnp.dot(own, own_hot_ref[i], preferred_element_type=F32) + jnp.dot(
                other, other_hot_ref[i], preferred_element_type=F32
            )
            rows = rows.astype(BF16)
            out_ref[0, cut * size : (cut + 1) * size] = rows[:size]
            out_ref[1, cut * size : (cut + 1) * size] = rows[size:]


def place_rows(own, other, own_hot, other_hot):
    vmem = pl.BlockSpec(memory_space=pltpu.VMEM)
    cuts = len(own)
    shape = jax.ShapeDtypeStruct((2, cuts * own[0].shape[1], own[0].shape[2]), BF16)
    count = own_hot.shape[0]
    return pl.pallas_call(
        functools.partial(place_kernel, cuts),
        out_shape=(shape,) * count,
        in_specs=[vmem] * (2 * cuts + 2),
        out_specs=(vmem,) * count,
        compiler_params=pltpu.CompilerParams(vmem_limit_bytes=24 * 2**20),
        name="place_rows",
    )(*own, *other, own_hot, other_hot)


def placements(row_maps, place, count, rows):
    own_map = lax.dynamic_index_in_dim(row_maps, lax.axis_index("front"), 0, keepdims=False)
    level = place // 2
    firsts = [place * rows, (count + place) * rows]
    for step in range(1, count // 2):
        far = level ^ step
        target = 2 * far + place % 2
        firsts.append(jnp.where(far < level, count + target, target) * rows)
    firsts = jnp.stack(firsts)
    targets = firsts[:, None] + jnp.arange(rows, dtype=jnp.int32)[None, :]

    def hot(device):
        mapped = lax.dynamic_slice_in_dim(own_map, device * rows, rows, 0)
        return (mapped[None, :, None] == targets[:, None, :]).astype(BF16)

    return hot(place), hot(place ^ 1)


def relay_body(lower_panel, inverse_cols, update_panel, pivot_rhs, update_rhs, row_maps, parent_rhs):
    shots = pivot_rhs.shape[2]
    upd_rows = update_panel.shape[2]
    count = lax.axis_size("panel")
    place = lax.axis_index("panel").astype(jnp.int32)
    level = place // 2
    spread_rows, chain_rows, swap_rows = spread_plan(count)

    def send(value, edges):
        return lax.ppermute(value, "panel", edges)

    place_ref = jnp.reshape(place, (1,))
    own_hot, other_hot = placements(row_maps, place, count, upd_rows)
    near, acc_l, acc_u, before = setup(place_ref, lower_panel, shots)
    passed, mine = solve_first(place_ref, pivot_rhs, inverse_cols)
    urgent = None
    came = []
    settled = [acc_u, acc_u]
    for hop in range(count):
        relays = {p: came[earlier][i] for p, (earlier, i) in RELAY.get(hop, {}).items()}
        if hop:
            after = [settled[hop]]
            passed, mine, before = solve(
                hop, place_ref, after, pivot_rhs, acc_l, near, inverse_cols, urgent, mine, before, relays
            )
        parts = [(mine, [hop if p == hop else -1 for p in range(count)])]
        if hop:
            parts.append((urgent, chain_rows[hop - 1]))
        for earlier in range(hop):
            for i, (_, _, use) in enumerate(SPREAD[earlier]):
                if use == hop:
                    parts.append((came[earlier][i], spread_rows[earlier][i]))
        if hop < len(CHAIN):
            urgent = send(passed, CHAIN[hop])
        came.append([])
        for value, edges, _ in SPREAD[hop]:
            if value not in (OWN, PREV):
                value = came[value[0]][value[1]]
            else:
                value = mine if value == OWN else before
            came[hop].append(send(value, edges))
        if hop + 1 < count:
            acc_l = accumulate(f"lower_{hop}", True, place_ref, parts, lower_panel, acc_l)
        acc_u = accumulate(f"update_{hop}", False, place_ref, parts, update_panel, acc_u)
        settled.append(acc_u)

    def cross(name, settled, blocks, keep, cuts):
        values = {}
        for earlier, rows in enumerate(spread_rows):
            for i, row in enumerate(rows):
                for p in range(count):
                    if row[p] == blocks[p % 2]:
                        values[p] = came[earlier][i]
        outs = pick(name, place_ref, settled, values, mine, keep, cuts)
        return [send(value, SWAP) for value in outs[:cuts]] + list(outs[cuts:])

    first, solved = cross("pick_first", settled[count], (count - 2, count - 3), True, 1)
    acc_u = accumulate("update_mid", False, place_ref, [(first, swap_rows[0])], update_panel, acc_u)
    seconds = cross("pick_second", settled[count + 1], (None, count - 1), False, PARTS)
    parts = [(came[-1][i], row) for i, row in enumerate(spread_rows[-1])]
    acc_u = accumulate("update_late", False, place_ref, parts, update_panel, acc_u)
    children = [
        accumulate(
            f"update_last_{i}", False, place_ref, [(second, swap_rows[1])], update_panel, acc_u, update_rhs, i
        )
        for i, second in enumerate(seconds)
    ]
    placed = place_rows(children, [send(child, SWAP) for child in children], own_hot, other_hot)
    sums = [placed[0].astype(F32), placed[1].astype(F32)]
    for step in range(1, count // 2):
        moved = send(placed[1 + step], [(p, p ^ (2 * step)) for p in range(count)]).astype(F32)
        below = (level ^ step) < level
        sums[0] = sums[0] + jnp.where(below, moved, 0.0)
        sums[1] = sums[1] + jnp.where(below, 0.0, moved)
    odd_front = lax.axis_index("front") % 2 == 1
    kept = jnp.where(odd_front, sums[1], sums[0])
    given = jnp.where(odd_front, sums[0], sums[1]).astype(BF16)
    sibling = lax.ppermute(given, "front", [(f, f ^ 1) for f in range(lax.axis_size("front"))])
    parent_out = parent_rhs[0] + kept + sibling.astype(F32)
    return (solved, parent_out[None])


def select_rows(block_rows, index_map, base, owned):
    targets = base + jnp.arange(owned, dtype=jnp.int32)
    placement = (index_map[:, None] == targets[None, :]).astype(BF16)
    return jnp.einsum("csu,ur->csr", block_rows, placement, preferred_element_type=F32)


def extend_add(child_update, row_maps, parent_f):
    upd_rows = child_update.shape[2]
    panel_count = lax.axis_size("panel")
    panel_number = lax.axis_index("panel")
    front_number = lax.axis_index("front")
    parity = front_number % 2
    sibling_front = front_number + 1 - 2 * parity
    my_base = (parity * panel_count + panel_number) * upd_rows
    own_map = lax.dynamic_index_in_dim(row_maps, front_number, 0, keepdims=False)
    sibling_map = lax.dynamic_index_in_dim(row_maps, sibling_front, 0, keepdims=False)
    gathered = lax.all_gather(child_update, "panel", axis=2, tiled=True)
    pairs = [(source, source ^ 1) for source in range(lax.axis_size("front"))]
    sibling = lax.ppermute(gathered, "front", pairs)
    assembled = select_rows(gathered, own_map, my_base, upd_rows) + select_rows(
        sibling, sibling_map, my_base, upd_rows
    )
    return parent_f + assembled


def complex_product(matrix, vector, pattern):
    real_part = jnp.einsum(pattern, matrix[0], vector[0], preferred_element_type=F32) - jnp.einsum(
        pattern, matrix[1], vector[1], preferred_element_type=F32
    )
    imag_part = jnp.einsum(pattern, matrix[0], vector[1], preferred_element_type=F32) + jnp.einsum(
        pattern, matrix[1], vector[0], preferred_element_type=F32
    )
    return jnp.stack([real_part, imag_part])


def summed_body(lower_panel, inverse_cols, update_panel, pivot_rhs, update_rhs, row_maps, parent_rhs):
    lower_f = lower_panel[0]
    pivot_f = pivot_rhs[0]
    own_rows = lower_f.shape[1]
    block_count = lower_f.shape[2] // CB
    panel_number = lax.axis_index("panel")
    owner_block = panel_number * own_rows // CB
    partial_sum = jnp.zeros((2, pivot_f.shape[1], own_rows), F32)
    blocks = []
    for block in range(block_count):
        first = block * CB
        residual = (pivot_f.astype(F32) - partial_sum).astype(BF16)
        block_term = complex_product(inverse_cols[0], residual, "ri,sr->si")
        block_term = jnp.where(owner_block == block, block_term, 0.0)
        block_value = lax.psum(block_term.astype(BF16), "panel")
        blocks.append(block_value)
        partial_sum = partial_sum + complex_product(lower_f[:, :, first : first + CB], block_value, "rc,sc->sr")
    solution_f = jnp.concatenate(blocks, axis=2)
    own_solution = lax.dynamic_slice_in_dim(solution_f, panel_number * own_rows, own_rows, 2)
    applied = complex_product(update_panel[0], solution_f, "rc,sc->sr")
    child_update = (update_rhs[0].astype(F32) - applied).astype(BF16)
    parent_out = extend_add(child_update, row_maps, parent_rhs[0])
    return (own_solution[None], parent_out[None])


def solution(mesh):
    in_specs = (
        P("front", None, "panel", None),
        P("front", None, "panel", None),
        P("front", None, "panel", None),
        P("front", None, None, "panel"),
        P("front", None, None, "panel"),
        P(),
        P("front", None, None, "panel"),
    )
    out_specs = (P("front", None, None, "panel"), P("front", None, None, "panel"))

    def run(lower_panel, *others):
        blocks = lower_panel.shape[3] // CB
        one_block = mesh.shape["panel"] == blocks == len(SWAP)
        body = relay_body if one_block else summed_body
        call = jax.shard_map(body, mesh=mesh, in_specs=in_specs, out_specs=out_specs, check_vma=False)
        return call(lower_panel, *others)

    return run
```

```python
import functools

import jax
import jax.numpy as jnp
import numpy as np
from jax import lax
from jax.experimental import pallas as pl
from jax.experimental.pallas import tpu as pltpu
from jax.sharding import PartitionSpec as P

CB = 512
F32 = jnp.float32
BF16 = jnp.bfloat16

SWAP = ((0, 1), (1, 0), (2, 3), (3, 2), (4, 5), (5, 4), (6, 7), (7, 6))
CHAIN = (
    SWAP,
    ((1, 2), (2, 3), (3, 0), (0, 1), (4, 5), (5, 4), (6, 7), (7, 6)),
    SWAP,
    ((3, 4), (4, 5), (5, 2), (2, 3), (0, 1), (1, 0), (6, 7), (7, 6)),
    SWAP,
    ((5, 6), (6, 7), (7, 4), (4, 5), (0, 1), (1, 0), (2, 3), (3, 2)),
    SWAP,
)
RELAY = {
    2: {4: (0, 1), 6: (0, 0)},
    4: {7: (1, 0)},
    6: {0: (5, 4), 2: (5, 3)},
}
OWN, PREV = "own", "prev"
SPREAD = (
    ((OWN, ((0, 6),), 1), (OWN, ((0, 4),), 1), (OWN, ((0, 2),), 1)),
    ((OWN, ((1, 7),), 2), (OWN, ((1, 5),), 2), ((0, 2), ((2, 3),), 2), (OWN, ((1, 3),), 2)),
    ((PREV, ((2, 4),), 3), (OWN, ((2, 4),), 3)),
    ((OWN, ((3, 5), (2, 6)), 4), ((2, 1), ((4, 5),), 4)),
    ((PREV, ((4, 6),), 5), (OWN, ((4, 6),), 5), (OWN, ((2, 0), (3, 1)), 5), ((3, 0), ((5, 7),), 5)),
    (
        (OWN, ((5, 7),), 6),
        ((4, 1), ((6, 7),), 6),
        ((3, 0), ((6, 7),), 6),
        (OWN, ((5, 3), (4, 2)), 6),
        (OWN, ((5, 1), (4, 0)), 6),
        ((4, 2), ((0, 1), (1, 0)), 6),
    ),
    ((OWN, ((6, 4),), 7), (OWN, ((6, 2),), 7), (OWN, ((6, 0),), 7)),
    ((OWN, ((7, 1),), 8), (OWN, ((7, 3),), 8), (OWN, ((7, 5),), 8)),
)


PARTS = 2


def spread_plan(count):
    have = [{p} for p in range(count)]

    def taken(edges, block_of):
        row = [-1] * count
        for source, dest in edges:
            block = block_of(source)
            if block is not None and block not in have[dest]:
                row[dest] = block
        return row

    def keep(row):
        for p, block in enumerate(row):
            if block >= 0:
                assert block not in have[p]
                have[p].add(block)

    chain = []
    spread = []
    for hop in range(count):
        if hop < len(CHAIN):

            def passed(p, hop=hop):
                if p in RELAY.get(hop, {}):
                    earlier, i = RELAY[hop][p]
                    return spread[earlier][i][p]
                return p if p <= hop else None

            row = taken(CHAIN[hop], passed)
            assert row[hop + 1] == hop
            keep(row)
            chain.append(row)
        rows = []
        for value, edges, _ in SPREAD[hop]:
            if value == OWN:
                row = taken(edges, lambda source: source)
            elif value == PREV:
                row = taken(edges, lambda source: source - 1)
            else:
                row = taken(edges, lambda source, value=value: spread[value[0]][value[1]][source])
            assert sum(block >= 0 for block in row) == len(edges)
            keep(row)
            rows.append(row)
        spread.append(rows)
    swaps = []
    for even, odd in ((count - 3, count - 2), (count - 1, None)):
        row = taken(SWAP, lambda source, even=even, odd=odd: even if source % 2 else odd)
        keep(row)
        swaps.append(row)
    assert all(held == set(range(count)) for held in have)
    for p in range(count):
        for hop, rows in enumerate(spread):
            for (_, _, use), row in zip(SPREAD[hop], rows):
                assert use > hop and (row[p] < 0 or row[p] > p or use < p)
        for hop, row in enumerate(chain):
            assert row[p] < 0 or row[p] > p or hop + 1 < p or (hop + 1 == p and row[p] == hop)
    return spread, chain, swaps


def stacked(value):
    return jnp.concatenate([value[0], value[1]], axis=0)


def turned_of(value):
    half = value.shape[0] // 2
    return jnp.concatenate([-value[half:], value[:half]], axis=0)


def apply_rows(value, matrix_real, matrix_imag):
    dims = (((1,), (1,)), ((), ()))
    return lax.dot_general(value, matrix_real, dims, preferred_element_type=F32) + lax.dot_general(
        turned_of(value), matrix_imag, dims, preferred_element_type=F32
    )


def apply_columns(value, matrix_real, matrix_imag):
    return jnp.dot(value, matrix_real, preferred_element_type=F32) + jnp.dot(
        turned_of(value), matrix_imag, preferred_element_type=F32
    )


def setup_kernel(place_ref, lower_ref, near_ref, acc_l_ref, acc_u_ref, zero_ref, sem):
    width = near_ref.shape[-1]
    block = jnp.maximum(place_ref[0] - 1, 0)
    columns = pl.ds(pl.multiple_of(block * width, width), width)
    copy = pltpu.make_async_copy(lower_ref.at[0, :, :, columns], near_ref, sem)
    copy.start()
    for ref in (acc_l_ref, acc_u_ref, zero_ref):
        ref[...] = jnp.zeros_like(ref)
    copy.wait()


def setup(place, lower, shots):
    rows = lower.shape[2]
    vmem = pl.BlockSpec(memory_space=pltpu.VMEM)
    acc = pltpu.VMEM((2, shots, rows), F32)
    return pl.pallas_call(
        setup_kernel,
        out_shape=(pltpu.VMEM((2, rows, CB), BF16), acc, acc, pltpu.VMEM((2, shots, CB), BF16)),
        in_specs=[pl.BlockSpec(memory_space=pltpu.SMEM), pl.BlockSpec(memory_space=pltpu.HBM)],
        out_specs=(vmem,) * 4,
        scratch_shapes=[pltpu.SemaphoreType.DMA(())],
        compiler_params=pltpu.CompilerParams(vmem_limit_bytes=46 * 2**20),
        name="setup",
    )(place, lower)


def first_kernel(place_ref, rhs_ref, inv_ref, out_ref, mine_ref):
    shots = out_ref.shape[1]

    @pl.when(place_ref[0] != 0)
    def _():
        out_ref[...] = jnp.zeros_like(out_ref)
        mine_ref[...] = jnp.zeros_like(mine_ref)

    @pl.when(place_ref[0] == 0)
    def _():
        term = apply_columns(stacked(rhs_ref[0]), inv_ref[0, 0], inv_ref[0, 1]).astype(BF16)
        for ref in (out_ref, mine_ref):
            ref[0] = term[:shots]
            ref[1] = term[shots:]


def solve_first(place, rhs, inv):
    vmem = pl.BlockSpec(memory_space=pltpu.VMEM)
    return pl.pallas_call(
        first_kernel,
        out_shape=(pltpu.VMEM(rhs.shape[1:], BF16),) * 2,
        in_specs=[pl.BlockSpec(memory_space=pltpu.SMEM), vmem, vmem],
        out_specs=(vmem,) * 2,
        compiler_params=pltpu.CompilerParams(vmem_limit_bytes=16 * 2**20),
        name="solve_0",
    )(place, rhs, inv)


def solve_kernel(hop, relays, settled, place_ref, *refs):
    rhs_ref, acc_ref, near_ref, inv_ref, urgent_ref, mine_in, before_in, *refs = refs[settled:]
    relay_refs, (out_ref, mine_ref, before_ref) = refs[: len(relays)], refs[len(relays) :]
    place = place_ref[0]
    shots = out_ref.shape[1]

    @pl.when(place != hop)
    def _():
        out_ref[...] = mine_in[...]
        mine_ref[...] = mine_in[...]
        before_ref[...] = before_in[...]

    for p, relay_ref in zip(relays, relay_refs):

        @pl.when(place == p)
        def _(relay_ref=relay_ref):
            out_ref[...] = relay_ref[...]

    @pl.when(place == hop)
    def _():
        residual = stacked(rhs_ref[0]).astype(F32) - stacked(acc_ref[...])
        residual = residual - apply_rows(stacked(urgent_ref[...]), near_ref[0], near_ref[1])
        term = apply_columns(residual.astype(BF16), inv_ref[0, 0], inv_ref[0, 1]).astype(BF16)
        for ref in (out_ref, mine_ref):
            ref[0] = term[:shots]
            ref[1] = term[shots:]
        before_ref[...] = urgent_ref[...]


def solve(hop, place, settled, rhs, acc, near, inv, urgent, mine, before, relays):
    vmem = pl.BlockSpec(memory_space=pltpu.VMEM)
    smem = pl.BlockSpec(memory_space=pltpu.SMEM)
    block = pltpu.VMEM(mine.shape, BF16)
    args = [rhs, acc, near, inv, urgent, mine, before, *relays.values()]
    return pl.pallas_call(
        functools.partial(solve_kernel, hop, tuple(relays), len(settled)),
        out_shape=(block,) * 3,
        in_specs=[smem] + [pl.BlockSpec(memory_space=pl.ANY)] * len(settled) + [vmem] * len(args),
        out_specs=(vmem,) * 3,
        compiler_params=pltpu.CompilerParams(vmem_limit_bytes=16 * 2**20),
        name=f"solve_{hop}",
    )(place, *settled, *args)


def gather_kernel(arrivals, left, part, place_ref, *refs):
    count = len(arrivals)
    parts = refs[:count]
    refs = refs[count:]
    final = part is not None
    if final:
        panel_ref, acc_in, rhs_ref, out_ref, buf, sems, acc_ref = refs
    else:
        panel_ref, acc_in, acc_ref, buf, sems = refs
    width = buf.shape[-1]
    shots = acc_ref.shape[1]
    place = place_ref[0]
    blocks = []
    for row in arrivals:
        block = jnp.int32(-1)
        for p, value in enumerate(row):
            if value >= 0 and (value < p or not left):
                block = jnp.where(place == p, value, block)
        blocks.append(block)

    def copy_of(i):
        columns = pl.ds(pl.multiple_of(jnp.maximum(blocks[i], 0) * width, width), width)
        return pltpu.make_async_copy(panel_ref.at[0, :, :, columns], buf.at[i], sems.at[i])

    for i in range(count):

        @pl.when(blocks[i] >= 0)
        def _(i=i):
            copy_of(i).start()

    rows = slice(part * shots, (part + 1) * shots) if final else slice(None)
    acc_ref[...] = acc_in[:, rows]
    for i in range(count):

        @pl.when(blocks[i] >= 0)
        def _(i=i):
            copy_of(i).wait()
            product = apply_rows(stacked(parts[i][...]), buf[i, 0], buf[i, 1])
            acc_ref[0] += product[:shots]
            acc_ref[1] += product[shots:]

    if final:
        out_ref[...] = (rhs_ref[0, :, rows].astype(F32) - acc_ref[...]).astype(BF16)


def accumulate(name, left, place, items, panel, acc, rhs=None, part=None):
    items = [item for item in items if not left or any(0 <= block < p for p, block in enumerate(item[1]))]
    if not items:
        return acc
    parts = [item[0] for item in items]
    count = len(parts)
    final = part is not None
    shape = (2, acc.shape[1] // PARTS, acc.shape[2]) if final else acc.shape
    vmem = pl.BlockSpec(memory_space=pltpu.VMEM)
    hbm = pl.BlockSpec(memory_space=pltpu.HBM)
    scratch = [pltpu.VMEM((count, 2, panel.shape[2], CB), BF16), pltpu.SemaphoreType.DMA((count,))]
    return pl.pallas_call(
        functools.partial(gather_kernel, [item[1] for item in items], left, part),
        out_shape=pltpu.VMEM(shape, BF16 if final else F32),
        in_specs=[pl.BlockSpec(memory_space=pltpu.SMEM)] + [vmem] * count + [hbm, vmem] + [vmem] * final,
        out_specs=vmem,
        scratch_shapes=scratch + [pltpu.VMEM(shape, F32)] * final,
        input_output_aliases={count + 2: 0} if left else {},
        compiler_params=pltpu.CompilerParams(vmem_limit_bytes=46 * 2**20),
        name=name,
    )(place, *parts, panel, acc, *([rhs] if final else []))


def pick_kernel(places, keep, place_ref, settled_ref, *refs):
    del settled_ref
    count = len(places)
    sems = refs[-1]
    out_refs = refs[count + 1 : -1]
    if keep:
        out_refs, kept_ref = out_refs[:-1], out_refs[-1]
        kept = pltpu.make_async_copy(refs[count], kept_ref.at[0], sems.at[len(out_refs)])
        kept.start()
    size = out_refs[0].shape[1]

    for p, ref in zip(places, refs):

        @pl.when(place_ref[0] == p)
        def _(ref=ref):
            copies = [
                pltpu.make_async_copy(ref.at[:, pl.ds(i * size, size)], out_ref, sems.at[i])
                for i, out_ref in enumerate(out_refs)
            ]
            for copy in copies:
                copy.start()
            for copy in copies:
                copy.wait()

    if keep:
        kept.wait()


def pick(name, place, settled, values, default, keep, cuts):
    count = lax.axis_size("panel")
    vmem = pl.BlockSpec(memory_space=pltpu.VMEM)
    anywhere = pl.BlockSpec(memory_space=pl.ANY)
    args = [values.get(p, default) for p in range(count)] + [default]
    shots = default.shape[1]
    out_shape = [pltpu.VMEM((2, shots // cuts, CB), default.dtype)] * cuts
    if keep:
        out_shape.append(jax.ShapeDtypeStruct((1, *default.shape), default.dtype))
    return pl.pallas_call(
        functools.partial(pick_kernel, tuple(range(count)), keep),
        out_shape=out_shape,
        in_specs=[pl.BlockSpec(memory_space=pltpu.SMEM)] + [anywhere] * (1 + len(args)),
        out_specs=[vmem] * cuts + [anywhere] * keep,
        scratch_shapes=[pltpu.SemaphoreType.DMA((cuts + 1,))],
        compiler_params=pltpu.CompilerParams(vmem_limit_bytes=16 * 2**20),
        name=name,
    )(place, settled, *args)


def place_kernel(cuts, *refs):
    own_refs, other_refs = refs[:cuts], refs[cuts : 2 * cuts]
    own_hot_ref, other_hot_ref = refs[2 * cuts : 2 * cuts + 2]
    out_refs = refs[2 * cuts + 2 :]
    size = own_refs[0].shape[1]
    for cut in range(cuts):
        own = stacked(own_refs[cut][...])
        other = stacked(other_refs[cut][...])
        for i, out_ref in enumerate(out_refs):
            rows = jnp.dot(own, own_hot_ref[i], preferred_element_type=F32) + jnp.dot(
                other, other_hot_ref[i], preferred_element_type=F32
            )
            rows = rows.astype(BF16)
            out_ref[0, cut * size : (cut + 1) * size] = rows[:size]
            out_ref[1, cut * size : (cut + 1) * size] = rows[size:]


def place_rows(own, other, own_hot, other_hot):
    vmem = pl.BlockSpec(memory_space=pltpu.VMEM)
    cuts = len(own)
    shape = jax.ShapeDtypeStruct((2, cuts * own[0].shape[1], own[0].shape[2]), BF16)
    count = own_hot.shape[0]
    return pl.pallas_call(
        functools.partial(place_kernel, cuts),
        out_shape=(shape,) * count,
        in_specs=[vmem] * (2 * cuts + 2),
        out_specs=(vmem,) * count,
        compiler_params=pltpu.CompilerParams(vmem_limit_bytes=24 * 2**20),
        name="place_rows",
    )(*own, *other, own_hot, other_hot)


def placements(row_maps, place, count, rows):
    own_map = lax.dynamic_index_in_dim(row_maps, lax.axis_index("front"), 0, keepdims=False)
    level = place // 2
    firsts = [place * rows, (count + place) * rows]
    for step in range(1, count // 2):
        far = level ^ step
        target = 2 * far + place % 2
        firsts.append(jnp.where(far < level, count + target, target) * rows)
    firsts = jnp.stack(firsts)
    targets = firsts[:, None] + jnp.arange(rows, dtype=jnp.int32)[None, :]

    def hot(device):
        mapped = lax.dynamic_slice_in_dim(own_map, device * rows, rows, 0)
        return (mapped[None, :, None] == targets[:, None, :]).astype(BF16)

    return hot(place), hot(place ^ 1)


def relay_body(lower_panel, inverse_cols, update_panel, pivot_rhs, update_rhs, row_maps, parent_rhs):
    shots = pivot_rhs.shape[2]
    upd_rows = update_panel.shape[2]
    count = lax.axis_size("panel")
    place = lax.axis_index("panel").astype(jnp.int32)
    level = place // 2
    spread_rows, chain_rows, swap_rows = spread_plan(count)

    def send(value, edges):
        return lax.ppermute(value, "panel", edges)

    place_ref = jnp.reshape(place, (1,))
    own_hot, other_hot = placements(row_maps, place, count, upd_rows)
    near, acc_l, acc_u, before = setup(place_ref, lower_panel, shots)
    passed, mine = solve_first(place_ref, pivot_rhs, inverse_cols)
    urgent = None
    came = []
    settled = [acc_u, acc_u]
    for hop in range(count):
        relays = {p: came[earlier][i] for p, (earlier, i) in RELAY.get(hop, {}).items()}
        if hop:
            after = [settled[hop]]
            passed, mine, before = solve(
                hop, place_ref, after, pivot_rhs, acc_l, near, inverse_cols, urgent, mine, before, relays
            )
        parts = [(mine, [hop if p == hop else -1 for p in range(count)])]
        if hop:
            parts.append((urgent, chain_rows[hop - 1]))
        for earlier in range(hop):
            for i, (_, _, use) in enumerate(SPREAD[earlier]):
                if use == hop:
                    parts.append((came[earlier][i], spread_rows[earlier][i]))
        if hop < len(CHAIN):
            urgent = send(passed, CHAIN[hop])
        came.append([])
        for value, edges, _ in SPREAD[hop]:
            if value not in (OWN, PREV):
                value = came[value[0]][value[1]]
            else:
                value = mine if value == OWN else before
            came[hop].append(send(value, edges))
        if hop + 1 < count:
            acc_l = accumulate(f"lower_{hop}", True, place_ref, parts, lower_panel, acc_l)
        acc_u = accumulate(f"update_{hop}", False, place_ref, parts, update_panel, acc_u)
        settled.append(acc_u)

    def cross(name, settled, blocks, keep, cuts):
        values = {}
        for earlier, rows in enumerate(spread_rows):
            for i, row in enumerate(rows):
                for p in range(count):
                    if row[p] == blocks[p % 2]:
                        values[p] = came[earlier][i]
        outs = pick(name, place_ref, settled, values, mine, keep, cuts)
        return [send(value, SWAP) for value in outs[:cuts]] + list(outs[cuts:])

    first, solved = cross("pick_first", settled[count], (count - 2, count - 3), True, 1)
    acc_u = accumulate("update_mid", False, place_ref, [(first, swap_rows[0])], update_panel, acc_u)
    seconds = cross("pick_second", settled[count + 1], (None, count - 1), False, PARTS)
    parts = [(came[-1][i], row) for i, row in enumerate(spread_rows[-1])]
    acc_u = accumulate("update_late", False, place_ref, parts, update_panel, acc_u)
    children = [
        accumulate(
            f"update_last_{i}", False, place_ref, [(second, swap_rows[1])], update_panel, acc_u, update_rhs, i
        )
        for i, second in enumerate(seconds)
    ]
    placed = place_rows(children, [send(child, SWAP) for child in children], own_hot, other_hot)
    sums = [placed[0].astype(F32), placed[1].astype(F32)]
    for step in range(1, count // 2):
        moved = send(placed[1 + step], [(p, p ^ (2 * step)) for p in range(count)]).astype(F32)
        below = (level ^ step) < level
        sums[0] = sums[0] + jnp.where(below, moved, 0.0)
        sums[1] = sums[1] + jnp.where(below, 0.0, moved)
    odd_front = lax.axis_index("front") % 2 == 1
    kept = jnp.where(odd_front, sums[1], sums[0])
    given = jnp.where(odd_front, sums[0], sums[1]).astype(BF16)
    sibling = lax.ppermute(given, "front", [(f, f ^ 1) for f in range(lax.axis_size("front"))])
    parent_out = parent_rhs[0] + kept + sibling.astype(F32)
    return (solved, parent_out[None])


def select_rows(block_rows, index_map, base, owned):
    targets = base + jnp.arange(owned, dtype=jnp.int32)
    placement = (index_map[:, None] == targets[None, :]).astype(BF16)
    return jnp.einsum("csu,ur->csr", block_rows, placement, preferred_element_type=F32)


def extend_add(child_update, row_maps, parent_f):
    upd_rows = child_update.shape[2]
    panel_count = lax.axis_size("panel")
    panel_number = lax.axis_index("panel")
    front_number = lax.axis_index("front")
    parity = front_number % 2
    sibling_front = front_number + 1 - 2 * parity
    my_base = (parity * panel_count + panel_number) * upd_rows
    own_map = lax.dynamic_index_in_dim(row_maps, front_number, 0, keepdims=False)
    sibling_map = lax.dynamic_index_in_dim(row_maps, sibling_front, 0, keepdims=False)
    gathered = lax.all_gather(child_update, "panel", axis=2, tiled=True)
    pairs = [(source, source ^ 1) for source in range(lax.axis_size("front"))]
    sibling = lax.ppermute(gathered, "front", pairs)
    assembled = select_rows(gathered, own_map, my_base, upd_rows) + select_rows(
        sibling, sibling_map, my_base, upd_rows
    )
    return parent_f + assembled


def complex_product(matrix, vector, pattern):
    real_part = jnp.einsum(pattern, matrix[0], vector[0], preferred_element_type=F32) - jnp.einsum(
        pattern, matrix[1], vector[1], preferred_element_type=F32
    )
    imag_part = jnp.einsum(pattern, matrix[0], vector[1], preferred_element_type=F32) + jnp.einsum(
        pattern, matrix[1], vector[0], preferred_element_type=F32
    )
    return jnp.stack([real_part, imag_part])


def summed_body(lower_panel, inverse_cols, update_panel, pivot_rhs, update_rhs, row_maps, parent_rhs):
    lower_f = lower_panel[0]
    pivot_f = pivot_rhs[0]
    own_rows = lower_f.shape[1]
    block_count = lower_f.shape[2] // CB
    panel_number = lax.axis_index("panel")
    owner_block = panel_number * own_rows // CB
    partial_sum = jnp.zeros((2, pivot_f.shape[1], own_rows), F32)
    blocks = []
    for block in range(block_count):
        first = block * CB
        residual = (pivot_f.astype(F32) - partial_sum).astype(BF16)
        block_term = complex_product(inverse_cols[0], residual, "ri,sr->si")
        block_term = jnp.where(owner_block == block, block_term, 0.0)
        block_value = lax.psum(block_term.astype(BF16), "panel")
        blocks.append(block_value)
        partial_sum = partial_sum + complex_product(lower_f[:, :, first : first + CB], block_value, "rc,sc->sr")
    solution_f = jnp.concatenate(blocks, axis=2)
    own_solution = lax.dynamic_slice_in_dim(solution_f, panel_number * own_rows, own_rows, 2)
    applied = complex_product(update_panel[0], solution_f, "rc,sc->sr")
    child_update = (update_rhs[0].astype(F32) - applied).astype(BF16)
    parent_out = extend_add(child_update, row_maps, parent_rhs[0])
    return (own_solution[None], parent_out[None])


def solution(mesh):
    in_specs = (
        P("front", None, "panel", None),
        P("front", None, "panel", None),
        P("front", None, "panel", None),
        P("front", None, None, "panel"),
        P("front", None, None, "panel"),
        P(),
        P("front", None, None, "panel"),
    )
    out_specs = (P("front", None, None, "panel"), P("front", None, None, "panel"))

    def run(lower_panel, *others):
        blocks = lower_panel.shape[3] // CB
        one_block = mesh.shape["panel"] == blocks == len(SWAP)
        body = relay_body if one_block else summed_body
        call = jax.shard_map(body, mesh=mesh, in_specs=in_specs, out_specs=out_specs, check_vma=False)
        return call(lower_panel, *others)

    return run
```
